128 devices in a mesh: seq: 32 (over y, x, core), head: 4 (over z).
Axes of the slice: x: 4, y: 4, z: 4, core: 2. Of those that a mesh axis runs over, the one named last changes fastest.
Arguments:
- queries: bfloat16 [32768, 2048], P('seq', 'head'), may hold values from -6 to 6
- keys: bfloat16 [32768, 2048], P('seq', 'head'), may hold values from -100 to 100
- values: bfloat16 [32768, 2048], P('seq', 'head'), may hold values from -16 to 16
- gates: float32 [32768, 16], P('seq', 'head'), may hold values from 0.05 to 1
- ridge: float32 [16], P('head'), may hold values from 0.25 to 4
- out_weight: bfloat16 [2048, 2048], P(None, 'head'), may hold values from -0.125 to 0.125
Outputs:
- partial_out: bfloat16 [4, 32768, 2048], P('head', 'seq')
The draws below stay inside these ranges and needn't reach their ends.
All inputs are finite; a program needn't handle non-finite values.
Results may differ from the reference program's by a relative error of at most 0.0049.
Values may be sent and summed in bfloat16 or wider, within the bound.
No kernel may reach another device: no remote copies, remote signals or barrier semaphores. Data moves between devices by JAX's collectives and lax.ppermute only.
A program may use at most 128 MiB of HBM per device.

```python
import math
import jax
import jax.numpy as jnp
from jax import lax

D = 2048
HEADS = 16
HD = 128
SPAN = 128
ITERS = 8
TOKENS = 32768
N_HEAD = 4


def key_value_pair(key):
    scale_key = jax.random.fold_in(key, 101)
    normal_key = jax.random.fold_in(key, 202)
    mixing_key = jax.random.fold_in(key, 303)
    noise_key = jax.random.fold_in(key, 404)
    columns = HEADS * HD
    spread = math.log(10.0)
    scales = jnp.exp(jax.random.uniform(scale_key, (columns,), jnp.float32, 0.0, spread))
    base = jax.random.normal(normal_key, (TOKENS, columns), jnp.float32)
    raw_keys = jnp.clip(base * scales, -100.0, 100.0)
    grouped = raw_keys.reshape(TOKENS, HEADS, HD)
    unit_keys = grouped * lax.rsqrt(jnp.sum(grouped * grouped, -1, keepdims=True) + 1e-06)
    mixing = jax.random.normal(mixing_key, (HEADS, HD, HD), jnp.float32)
    mapped = jnp.einsum('thd,hde->the', unit_keys, mixing)
    noisy = mapped + 0.7 * jax.random.normal(noise_key, (TOKENS, HEADS, HD), jnp.float32)
    return (raw_keys, jnp.clip(noisy, -16.0, 16.0).reshape(TOKENS, columns))


def draw_keys(key, part):
    return key_value_pair(key)[0].astype(jnp.bfloat16)


def draw_values(key, part):
    return key_value_pair(key)[1].astype(jnp.bfloat16)


def block_scale(rng, shape, pieces, least, high):
    gain, own = 1.0, jax.random.fold_in(rng, 6)
    for axis_at, shards_of in pieces:
        heights = jnp.exp(jax.random.uniform(jax.random.fold_in(own, axis_at), (shards_of,), jnp.float32, least / len(pieces), high / len(pieces)))
        gain = gain * jnp.repeat(heights, shape[axis_at] // shards_of).reshape([-1 if axis == axis_at else 1 for axis in range(len(shape))])
    return gain


def normal_values(key, shape, deviation, bound, cuts=(), held_as=jnp.bfloat16):
    factor_of = block_scale(key, shape, cuts, -0.22, 0.18) if cuts else 1.0
    result = jax.random.normal(key, shape, jnp.float32) * deviation * factor_of
    return jnp.minimum(jnp.maximum(result, -bound), bound).astype(held_as)


def setup_inputs(seed: int = 0) -> dict:
    streams_of = jax.random.split(jax.random.key(seed), 7)
    return {
        "queries": normal_values(streams_of[0], (TOKENS, HEADS * HD), 1.0, 6.0, ((0, 32), (1, 4))),
        "keys": draw_keys(jax.random.fold_in(streams_of[6], 71), 0),
        "values": draw_values(jax.random.fold_in(streams_of[6], 71), 0),
        "gates": jnp.clip(jnp.exp(math.log(1.0) - 2.9957323 * jax.random.uniform(streams_of[3], (TOKENS, HEADS), jnp.float32) ** block_scale(streams_of[3], (TOKENS, HEADS), ((0, 32), (1, 4)), -0.2, 0.2)), 0.05, 1.0),
        "ridge": jnp.clip(jnp.exp(math.log(4.0) - 2.7725887 * jax.random.uniform(streams_of[4], (HEADS,), jnp.float32) ** block_scale(streams_of[4], (HEADS,), ((0, 4),), -0.2, 0.2)), 0.25, 4.0),
        "out_weight": normal_values(streams_of[5], (HEADS * HD, D), (HEADS * HD) ** -0.5, 0.125, ((1, 4),)),
    }


highest = lax.Precision.HIGHEST

def unit_rows(matrix):
    return matrix * lax.rsqrt(lax.optimization_barrier(jnp.sum(matrix * matrix, -1, keepdims=True)) + 1e-06)

def solve_block(prior_gram, prior_moment, keys_unit, keys_gated, values_gated, queries_unit, ridge_column, causal_mask):

    def apply_system(direction):
        from_prior = jnp.einsum('...de,...te->...td', prior_gram, direction, precision=highest)
        correlations = jnp.einsum('...id,...td->...ti', keys_unit, direction, precision=highest) * causal_mask
        from_block = jnp.einsum('...ti,...id->...td', correlations, keys_gated, precision=highest)
        return from_prior + from_block + ridge_column * direction

    def sweep_once(sweep, state):
        solution, residual, direction, norm_now = state
        image = apply_system(direction)
        step_size = norm_now / (lax.optimization_barrier(jnp.sum(direction * image, -1, keepdims=True)) + 1e-06)
        solution = solution + step_size * direction
        residual = residual - step_size * image
        norm_next = lax.optimization_barrier(jnp.sum(residual * residual, -1, keepdims=True))
        direction = residual + norm_next / (norm_now + 1e-06) * direction
        return (solution, residual, direction, norm_next)
    start_state = (jnp.zeros_like(queries_unit), queries_unit, queries_unit, lax.optimization_barrier(jnp.sum(queries_unit * queries_unit, -1, keepdims=True)))
    solution = lax.fori_loop(0, ITERS, sweep_once, start_state)[0]
    correlations = jnp.einsum('...id,...td->...ti', keys_unit, solution, precision=highest) * causal_mask
    readout = jnp.einsum('...ed,...td->...te', prior_moment, solution, precision=highest)
    return readout + jnp.einsum('...ti,...ie->...te', correlations, values_gated, precision=highest)

def reference(queries, keys, values, gates, ridge, out_weight):
    blocks = TOKENS // SPAN

    def split(matrix):
        return matrix.astype(jnp.float32).reshape(blocks, SPAN, HEADS, HD).transpose(0, 2, 1, 3)
    queries_unit = unit_rows(split(queries))
    keys_unit = unit_rows(split(keys))
    gate_cols = gates.astype(jnp.float32).reshape(blocks, SPAN, HEADS).transpose(0, 2, 1)[..., None]
    keys_gated = keys_unit * gate_cols
    values_gated = split(values) * gate_cols
    positions = jnp.arange(SPAN)
    causal_mask = (positions[None, :] <= positions[:, None]).astype(jnp.float32)
    ridge_column = ridge.astype(jnp.float32)[:, None, None]

    def advance(carry, block):
        prior_gram, prior_moment = carry
        unit_block, gated_block, value_block, query_block = block
        readout = solve_block(prior_gram, prior_moment, unit_block, gated_block, value_block, query_block, ridge_column, causal_mask)
        prior_gram = prior_gram + jnp.einsum('hid,hie->hde', gated_block, unit_block, precision=highest)
        prior_moment = prior_moment + jnp.einsum('hie,hid->hed', value_block, unit_block, precision=highest)
        return ((prior_gram, prior_moment), readout)
    zeros = jnp.zeros((HEADS, HD, HD), jnp.float32)
    _, readouts = lax.scan(advance, (zeros, zeros), (keys_unit, keys_gated, values_gated, queries_unit))
    readout = readouts.transpose(0, 2, 1, 3).reshape(TOKENS, HEADS * HD).astype(jnp.bfloat16)
    group_width = HEADS * HD // N_HEAD
    slabs = []
    for group in range(N_HEAD):
        lower = group * group_width
        slabs.append(jnp.dot(readout[:, lower:lower + group_width], out_weight[lower:lower + group_width], preferred_element_type=jnp.float32))
    return jnp.stack(slabs).astype(jnp.bfloat16)
```

```python
import functools
import jax
import jax.numpy as jnp
from jax import lax
from jax.experimental import pallas as pl
from jax.experimental.pallas import tpu as pltpu
from jax.sharding import PartitionSpec as P

HD = 128
SPAN = 128
ITERS = 8
EPS = 1e-06
F32 = jnp.float32
BF16 = jnp.bfloat16
F16 = jnp.float16
VMEM_LIMIT = 56 * 1024 * 1024


def two_terms(value):
    high = value.astype(BF16)
    return high, (value - high.astype(F32)).astype(BF16)


def dot(left, right):
    return jnp.dot(left, right, preferred_element_type=F32)


def dot_rows(left, right):
    return lax.dot_general(left, right, (((0,), (0,)), ((), ())), preferred_element_type=F32)


def key_norms(keys):
    return jnp.sum(keys * keys, axis=1, keepdims=True) + EPS


def head_cols(head):
    return slice(head * HD, (head + 1) * HD)


def totals_kernel(heads, core_ref, keys_ref, gates_ref, mine_ref, theirs_ref):
    core = core_ref[0]
    half = heads // 2
    for head in range(heads):
        block = keys_ref[:, head_cols(head)]
        keys = block.astype(F32)
        scaled = keys * (gates_ref[:, head : head + 1] / key_norms(keys))
        high, low = two_terms(scaled)
        product = dot_rows(block, jnp.concatenate([high, low], axis=1))
        gram = product[:, :HD] + product[:, HD:]

        @pl.when(core == head // half)
        def _():
            mine_ref[head % half] = gram

        @pl.when(core != head // half)
        def _():
            theirs_ref[head % half] = gram


def local_kernel(
    heads, blocks, keys_ref, values_ref, gates_ref, gram_ref, moment_ref, total_ref, gram_sum, moment_sum
):
    step = pl.program_id(0)

    @pl.when(step == 0)
    def _():
        gram_sum[...] = jnp.zeros_like(gram_sum)
        moment_sum[...] = jnp.zeros_like(moment_sum)

    for head in range(heads):
        block = keys_ref[:, head_cols(head)]
        keys = block.astype(F32)
        inverse = lax.rsqrt(key_norms(keys))
        gated = keys * (gates_ref[:, head : head + 1] * inverse)
        gram_high, gram_low = two_terms(gated * inverse)
        high, low = two_terms(gated)
        product = dot_rows(block, jnp.concatenate([gram_high, gram_low], axis=1))
        gram_ref[head, 0] = gram_sum[head]
        gram_sum[head] += product[:, :HD] + product[:, HD:]
        product = dot_rows(values_ref[:, head_cols(head)], jnp.concatenate([high, low], axis=1))
        moment_ref[head, 0] = moment_sum[head]
        moment_sum[head] += product[:, :HD] + product[:, HD:]

    @pl.when(step == blocks - 1)
    def _():
        total_ref[...] = moment_sum[...].astype(BF16)


def solve_kernel(
    heads,
    blocks,
    core_ref,
    ridge_ref,
    queries_ref,
    keys_ref,
    gates_ref,
    local_ref,
    keep_ref,
    got_ref,
    high_ref,
    low_ref,
    corr_ref,
    first,
    second,
    weights,
    xs,
    rs,
    ds,
    norms,
):
    core = core_ref[0]
    half = heads // 2
    row = lax.broadcasted_iota(jnp.int32, (SPAN, SPAN), 0)
    column = lax.broadcasted_iota(jnp.int32, (SPAN, SPAN), 1)
    causal = row <= column
    units = [(head, block) for block in range(blocks) for head in range(heads)]
    for unit, (head, block) in enumerate(units):
        rows = slice(block * SPAN, (block + 1) * SPAN)
        own = keys_ref[rows, head_cols(head)]
        keys = own.astype(F32)
        norm = key_norms(keys)
        weights[unit] = jnp.where(causal, gates_ref[rows, head : head + 1] / norm, 0.0)
        prior = jnp.where(core == head // half, keep_ref[head % half], got_ref[head % half])
        gram = prior + local_ref[head, block] + jnp.where(row == column, ridge_ref[head], 0.0)
        high, low = two_terms(gram)
        first[unit, :HD, :HD] = high
        first[unit, :HD, HD:] = high
        first[unit, HD:, :HD] = own
        first[unit, HD:, HD:] = own
        second[unit, :, :HD] = low
        second[unit, :, HD:] = keys.T.astype(BF16)
        query = queries_ref[rows, head_cols(head)].astype(F32).T
        query = query * lax.rsqrt(jnp.sum(query * query, axis=0, keepdims=True) + EPS)
        xs[unit] = jnp.zeros((HD, SPAN), F32)
        rs[unit] = query
        ds[unit] = query
        norms[unit] = jnp.broadcast_to(jnp.sum(query * query, axis=0, keepdims=True), (8, SPAN))

    def sweep_once(sweep, carry):
        for unit in range(len(units)):
            direction = ds[unit]
            now = norms[unit, :1]
            high, low = two_terms(direction)
            product = dot(first[unit], jnp.concatenate([high, low], axis=0))
            corr = (product[HD:] * weights[unit]).astype(BF16)
            image = product[:HD] + dot(second[unit], jnp.concatenate([high, corr], axis=0))
            step = now / (jnp.sum(direction * image, axis=0, keepdims=True) + EPS)
            xs[unit] += step * direction
            residual = rs[unit] - step * image
            rs[unit] = residual
            after = jnp.sum(residual * residual, axis=0, keepdims=True)
            ds[unit] = residual + (after / (now + EPS)) * direction
            norms[unit] = jnp.broadcast_to(after, (8, SPAN))
        return carry

    lax.fori_loop(0, ITERS, sweep_once, 0)
    for unit, (head, block) in enumerate(units):
        rows = slice(block * SPAN, (block + 1) * SPAN)
        high, low = two_terms(xs[unit])
        norm = key_norms(keys_ref[rows, head_cols(head)].astype(F32))
        corr = dot(first[unit, HD:], jnp.concatenate([high, low], axis=0))
        scale = jnp.where(causal, gates_ref[rows, head : head + 1] * lax.rsqrt(norm), 0.0)
        high_ref[head, :, rows] = high
        low_ref[head, :, rows] = low
        corr_ref[head, :, rows] = (corr * scale).astype(BF16)


def project_kernel(
    heads,
    blocks,
    groups,
    group_ref,
    values_ref,
    high_ref,
    low_ref,
    corr_ref,
    local_ref,
    prior_ref,
    own_ref,
    *rest,
):
    others, out_ref = rest[: groups - 1], rest[groups - 1]
    readout = rest[groups]
    for block in range(blocks):
        rows = slice(block * SPAN, (block + 1) * SPAN)
        for head in range(heads):
            moment_high, moment_low = two_terms(prior_ref[head] + local_ref[head, block])
            values = values_ref[rows, head_cols(head)].astype(F32).T.astype(BF16)
            left = jnp.concatenate([moment_high, moment_high, moment_low, values], axis=1)
            high = high_ref[head, :, rows]
            right = jnp.concatenate([high, low_ref[head, :, rows], high, corr_ref[head, :, rows]], axis=0)
            readout[rows, head_cols(head)] = dot(left, right).T.astype(BF16)
    group = group_ref[0]
    width = own_ref.shape[1]
    for shift, part in enumerate((own_ref,) + tuple(others)):
        source = lax.rem(group + groups - shift, groups)
        columns = pl.ds(pl.multiple_of(source * width, width), width)
        out_ref[0, :, columns] = dot(readout[...], part[...]).astype(BF16)


def params():
    return pltpu.CompilerParams(vmem_limit_bytes=VMEM_LIMIT)


def whole(shape):
    return pl.BlockSpec(shape, lambda *a: (0,) * len(shape))


def shards(mesh, queries, keys, values, gates, ridge, out_weight):
    tokens, width = queries.shape
    heads = width // HD
    half = heads // 2
    blocks = tokens // SPAN
    seq, groups = mesh.shape["seq"], mesh.shape["head"]
    columns = out_weight.shape[1]
    side = 4
    place = lax.axis_index("seq")
    core = lax.rem(place, 2)
    x_at = lax.rem(place // 2, side)
    y_at = place // (2 * side)
    group = lax.axis_index("head")
    core_arg = core.reshape(1).astype(jnp.int32)
    group_arg = group.reshape(1).astype(jnp.int32)
    smem = pl.BlockSpec(memory_space=pltpu.SMEM)

    def perm_core():
        return [(p, p ^ 1) for p in range(seq)]

    def perm_x(shift):
        return [(p, (p // 8) * 8 + ((p // 2 + shift) % side) * 2 + p % 2) for p in range(seq)]

    def perm_y(shift):
        return [(p, (p + 8 * shift) % seq) for p in range(seq)]

    def send(array, perm):
        return lax.ppermute(array, "seq", perm)

    parts = []
    for shift in range(1, groups):
        to = lax.rem(group + shift, groups)
        piece = lax.dynamic_slice_in_dim(out_weight, to * width, width, 0)
        parts.append(
            lax.ppermute(piece, "head", [(i, (i + shift) % groups) for i in range(groups)])
        )

    square = (half, HD, HD)
    mine, theirs = pl.pallas_call(
        functools.partial(totals_kernel, heads),
        in_specs=[smem, pl.BlockSpec(memory_space=pltpu.VMEM), pl.BlockSpec(memory_space=pltpu.VMEM)],
        out_specs=[pl.BlockSpec(memory_space=pltpu.VMEM)] * 2,
        out_shape=[jax.ShapeDtypeStruct(square, F32)] * 2,
        compiler_params=params(),
        cost_estimate=pl.CostEstimate(
            flops=4 * tokens * width * HD, bytes_accessed=2 * tokens * width, transcendentals=0
        ),
        name="totals",
    )(core_arg, keys, gates)

    local_gram, local_moment, moment_total = pl.pallas_call(
        functools.partial(local_kernel, heads, blocks),
        grid=(blocks,),
        in_specs=[
            pl.BlockSpec((SPAN, width), lambda b: (b, 0)),
            pl.BlockSpec((SPAN, width), lambda b: (b, 0)),
            pl.BlockSpec((SPAN, heads), lambda b: (b, 0)),
        ],
        out_specs=[
            pl.BlockSpec((heads, 1, HD, HD), lambda b: (0, b, 0, 0)),
            pl.BlockSpec((heads, 1, HD, HD), lambda b: (0, b, 0, 0)),
            whole((heads, HD, HD)),
        ],
        out_shape=[
            jax.ShapeDtypeStruct((heads, blocks, HD, HD), F32),
            jax.ShapeDtypeStruct((heads, blocks, HD, HD), F32),
            jax.ShapeDtypeStruct((heads, HD, HD), BF16),
        ],
        scratch_shapes=[pltpu.VMEM((heads, HD, HD), F32)] * 2,
        compiler_params=params(),
        cost_estimate=pl.CostEstimate(
            flops=8 * tokens * width * HD, bytes_accessed=12 * tokens * width, transcendentals=0
        ),
        name="local",
    )(keys, values, gates)

    received = send(theirs, perm_core())
    chip = (mine + received).astype(F16)
    along = [send(chip, perm_x(shift)) for shift in range(1, side)]
    wide = [part.astype(F32) for part in along]
    row_total = (chip.astype(F32) + wide[0] + wide[1] + wide[2]).astype(F16)
    row_before = sum(jnp.where(x_at >= shift, part, 0.0) for shift, part in enumerate(wide, 1))
    above = [send(row_total, perm_y(shift)).astype(F32) for shift in range(1, side)]
    before = row_before + sum(jnp.where(y_at >= shift, part, 0.0) for shift, part in enumerate(above, 1))
    keep = before + jnp.where(core == 1, received, 0.0)
    give = before + jnp.where(core == 0, mine, 0.0)
    got = send(give, perm_core())

    other = send(moment_total, perm_core())
    moment_core = jnp.where(core == 1, other, jnp.zeros_like(other)).astype(F32)
    moment_chip = (moment_total.astype(F32) + other.astype(F32)).astype(BF16)
    wide = [send(moment_chip, perm_x(shift)).astype(F32) for shift in range(1, side)]
    row_total = (moment_chip.astype(F32) + wide[0] + wide[1] + wide[2]).astype(BF16)
    row_before = sum(jnp.where(x_at >= shift, part, 0.0) for shift, part in enumerate(wide, 1))
    above = [send(row_total, perm_y(shift)).astype(F32) for shift in range(1, side)]
    moment_prior = (
        moment_core
        + row_before
        + sum(jnp.where(y_at >= shift, part, 0.0) for shift, part in enumerate(above, 1))
    )

    step_blocks = 2
    step = step_blocks * SPAN
    units = heads * step_blocks
    calls = 2
    solved = []
    for call in range(calls):
        grid = blocks // step_blocks // calls
        base = call * grid
        solved.append(
            pl.pallas_call(
                functools.partial(solve_kernel, heads, step_blocks),
                grid=(grid,),
                in_specs=[
                    smem,
                    smem,
                    pl.BlockSpec((step, width), lambda b, base=base: (b + base, 0)),
                    pl.BlockSpec((step, width), lambda b, base=base: (b + base, 0)),
                    pl.BlockSpec((step, heads), lambda b, base=base: (b + base, 0)),
                    pl.BlockSpec((heads, step_blocks, HD, HD), lambda b, base=base: (0, b + base, 0, 0)),
                    whole(square),
                    whole(square),
                ],
                out_specs=[pl.BlockSpec((heads, HD, step), lambda b: (0, 0, b))] * 3,
                out_shape=[jax.ShapeDtypeStruct((heads, HD, tokens // calls), BF16)] * 3,
                scratch_shapes=[
                    pltpu.VMEM((units, 2 * HD, 2 * HD), BF16),
                    pltpu.VMEM((units, HD, 2 * HD), BF16),
                    pltpu.VMEM((units, SPAN, SPAN), F32),
                    pltpu.VMEM((units, HD, SPAN), F32),
                    pltpu.VMEM((units, HD, SPAN), F32),
                    pltpu.VMEM((units, HD, SPAN), F32),
                    pltpu.VMEM((units, 8, SPAN), F32),
                ],
                compiler_params=params(),
                cost_estimate=pl.CostEstimate(
                    flops=48 * ITERS * tokens * width * HD // calls,
                    bytes_accessed=20 * tokens * width // calls,
                    transcendentals=0,
                ),
                name="solve",
            )(core_arg, ridge, queries, keys, gates, local_gram, keep, got)
        )
    high, low, corr = (jnp.concatenate(group_of, axis=2) for group_of in zip(*solved))

    out = pl.pallas_call(
        functools.partial(project_kernel, heads, step_blocks, groups),
        grid_spec=pltpu.PrefetchScalarGridSpec(
            num_scalar_prefetch=1,
            grid=(blocks // step_blocks,),
            in_specs=[
                pl.BlockSpec((step, width), lambda b, g: (b, 0)),
                pl.BlockSpec((heads, HD, step), lambda b, g: (0, 0, b)),
                pl.BlockSpec((heads, HD, step), lambda b, g: (0, 0, b)),
                pl.BlockSpec((heads, HD, step), lambda b, g: (0, 0, b)),
                pl.BlockSpec((heads, step_blocks, HD, HD), lambda b, g: (0, b, 0, 0)),
                whole((heads, HD, HD)),
                pl.BlockSpec((width, columns), lambda b, g: (g[0], 0)),
            ]
            + [whole((width, columns))] * (groups - 1),
            out_specs=pl.BlockSpec((1, step, columns * groups), lambda b, g: (0, b, 0)),
            scratch_shapes=[pltpu.VMEM((step, width), BF16)],
        ),
        out_shape=jax.ShapeDtypeStruct((1, tokens, columns * groups), BF16),
        compiler_params=params(),
        cost_estimate=pl.CostEstimate(
            flops=2 * tokens * width * columns * groups,
            bytes_accessed=24 * tokens * width,
            transcendentals=0,
        ),
        name="project",
    )(group_arg, values, high, low, corr, local_moment, moment_prior, out_weight, *parts)
    return out


def solution(mesh):
    return jax.shard_map(
        functools.partial(shards, mesh),
        mesh=mesh,
        in_specs=(
            P("seq", "head"),
            P("seq", "head"),
            P("seq", "head"),
            P("seq", "head"),
            P("head"),
            P(None, "head"),
        ),
        out_specs=P("head", "seq", None),
        check_vma=False,
    )
```

```python
import functools
import jax
import jax.numpy as jnp
from jax import lax
from jax.experimental import pallas as pl
from jax.experimental.pallas import tpu as pltpu
from jax.sharding import PartitionSpec as P

HD = 128
SPAN = 128
ITERS = 8
EPS = 1e-06
F32 = jnp.float32
BF16 = jnp.bfloat16
F16 = jnp.float16
VMEM_LIMIT = 56 * 1024 * 1024


def two_terms(value):
    high = value.astype(BF16)
    return high, (value - high.astype(F32)).astype(BF16)


def dot(left, right):
    return jnp.dot(left, right, preferred_element_type=F32)


def head_cols(head):
    return slice(head * HD, (head + 1) * HD)


def totals_kernel(half, core_ref, keys_ref, gates_ref, mine_ref, theirs_ref, turned_ref, scale_ref, gated_ref):
    head = pl.program_id(0)
    block = keys_ref[...]
    turned = block.T
    turned_ref[0] = turned
    wide = turned.astype(F32)
    norm = jnp.sum(wide * wide, axis=0, keepdims=True) + EPS
    gate = gates_ref[pl.ds(head, 1), :]
    scale = gate / norm
    scale_ref[0] = scale
    gated_ref[0] = gate * lax.rsqrt(norm)
    high, low = two_terms(wide * scale)
    product = dot(jnp.concatenate([high, low], axis=0), block)
    gram = product[:HD] + product[HD:]
    own = core_ref[0] == head // half

    @pl.when(own)
    def _():
        mine_ref[lax.rem(head, half)] = gram

    @pl.when(jnp.logical_not(own))
    def _():
        theirs_ref[lax.rem(head, half)] = gram


def moment_kernel(turned_ref, gated_ref, values_ref, total_ref):
    high, low = two_terms(turned_ref[0].astype(F32) * gated_ref[0])
    product = dot(jnp.concatenate([high, low], axis=0), values_ref[...])
    total_ref[0] = (product[:HD] + product[HD:]).astype(BF16)


def local_kernel(blocks, turned_ref, scale_ref, gated_ref, keys_ref, values_ref, gram_ref, moment_ref, values_turned_ref):
    values_turned_ref[0] = values_ref[...].T
    gram_ref[0, 0] = jnp.zeros((HD, HD), F32)
    moment_ref[0, 0] = jnp.zeros((HD, HD), F32)
    for block in range(blocks - 1):
        span = slice(block * SPAN, (block + 1) * SPAN)
        keys = turned_ref[0, :, span].astype(F32)
        high, low = two_terms(keys * scale_ref[0, :, span])
        product = dot(jnp.concatenate([high, low], axis=0), keys_ref[span, :])
        gram_ref[0, block + 1] = gram_ref[0, block] + (product[:HD] + product[HD:])
        high, low = two_terms(keys * gated_ref[0, :, span])
        product = dot(jnp.concatenate([high, low], axis=0), values_ref[span, :])
        moment_ref[0, block + 1] = moment_ref[0, block] + (product[:HD] + product[HD:]).T


def masks_kernel(blocks, queries_ref, scale_ref, gated_ref, turned_ref, gram_mask_ref, moment_mask_ref):
    row = lax.broadcasted_iota(jnp.int32, (SPAN, SPAN), 0)
    column = lax.broadcasted_iota(jnp.int32, (SPAN, SPAN), 1)
    turned_ref[0] = queries_ref[...].T
    for block in range(blocks):
        span = slice(block * SPAN, (block + 1) * SPAN)
        for out_ref, factors in ((gram_mask_ref, scale_ref), (moment_mask_ref, gated_ref)):
            factor = jnp.broadcast_to(factors[0, :, span], (SPAN, SPAN)).T
            out_ref[0, block] = jnp.where(row <= column, factor, 0.0)


def solve_kernel(
    heads,
    blocks,
    core_ref,
    ridge_ref,
    queries_ref,
    keys_ref,
    turned_ref,
    gram_mask_ref,
    moment_mask_ref,
    local_ref,
    keep_ref,
    got_ref,
    high_ref,
    low_ref,
    corr_ref,
    first,
    second,
    xs,
    rs,
    ds,
    norms,
):
    core = core_ref[0]
    half = heads // 2
    row = lax.broadcasted_iota(jnp.int32, (SPAN, SPAN), 0)
    column = lax.broadcasted_iota(jnp.int32, (SPAN, SPAN), 1)
    units = [(head, block) for block in range(blocks) for head in range(heads)]
    count = len(units)
    for head in range(heads):
        prior = jnp.where(core == head // half, keep_ref[head % half], got_ref[head % half])
        prior = prior + jnp.where(row == column, ridge_ref[head], 0.0)
        for block in range(blocks):
            unit = block * heads + head
            rows = slice(block * SPAN, (block + 1) * SPAN)
            own = keys_ref[rows, head_cols(head)]
            high, low = two_terms(prior + local_ref[head, block])
            first[unit, :HD, :HD] = high
            first[unit, :HD, HD:] = high
            first[unit, HD:, :HD] = own
            first[unit, HD:, HD:] = own
            second[unit, :, :HD] = low
            second[unit, :, HD:] = turned_ref[head, :, rows]
            query = queries_ref[head, :, rows].astype(F32)
            query = query * lax.rsqrt(jnp.sum(query * query, axis=0, keepdims=True) + EPS)
            xs[unit] = jnp.zeros((HD, SPAN), F32)
            rs[unit] = query
            ds[unit] = query
            norms[unit] = jnp.sum(query * query, axis=0, keepdims=True)

    def product_of(unit):
        high, low = two_terms(ds[unit])
        return high, dot(first[unit], jnp.concatenate([high, low], axis=0))

    def image_of(unit, high, product):
        head, block = units[unit]
        corr = (product[HD:] * gram_mask_ref[head, block]).astype(BF16)
        return product[:HD] + dot(second[unit], jnp.concatenate([high, corr], axis=0))

    def update(unit, image):
        direction = ds[unit]
        now = norms[unit]
        step = now / (jnp.sum(direction * image, axis=0, keepdims=True) + EPS)
        xs[unit] += step * direction
        residual = rs[unit] - step * image
        rs[unit] = residual
        after = jnp.sum(residual * residual, axis=0, keepdims=True)
        ds[unit] = residual + (after / (now + EPS)) * direction
        norms[unit] = after

    lag = 4

    def sweep_once(sweep, carry):
        products, images = {}, {}
        for at in range(count + 2 * lag):
            if at < count:
                products[at] = product_of(at)
            if 0 <= at - lag < count:
                images[at - lag] = image_of(at - lag, *products.pop(at - lag))
            if 0 <= at - 2 * lag < count:
                update(at - 2 * lag, images.pop(at - 2 * lag))
        return carry

    lax.fori_loop(0, ITERS, sweep_once, 0)
    for unit, (head, block) in enumerate(units):
        rows = slice(block * SPAN, (block + 1) * SPAN)
        high, low = two_terms(xs[unit])
        corr = dot(first[unit, HD:], jnp.concatenate([high, low], axis=0))
        high_ref[head, :, rows] = high
        low_ref[head, :, rows] = low
        corr_ref[head, :, rows] = (corr * moment_mask_ref[head, block]).astype(BF16)


def project_kernel(
    heads,
    blocks,
    groups,
    group_ref,
    values_ref,
    high_ref,
    low_ref,
    corr_ref,
    local_ref,
    prior_ref,
    own_ref,
    *rest,
):
    others, out_ref = rest[: groups - 1], rest[groups - 1]
    readout = rest[groups]
    for head in range(heads):
        prior = prior_ref[head].T
        for block in range(blocks):
            rows = slice(block * SPAN, (block + 1) * SPAN)
            moment_high, moment_low = two_terms(prior + local_ref[head, block])
            left = jnp.concatenate([moment_high, moment_high, moment_low, values_ref[head, :, rows]], axis=1)
            high = high_ref[head, :, rows]
            right = jnp.concatenate([high, low_ref[head, :, rows], high, corr_ref[head, :, rows]], axis=0)
            readout[rows, head_cols(head)] = dot(left, right).T.astype(BF16)
    group = group_ref[0]
    width = own_ref.shape[1]
    for shift, part in enumerate((own_ref,) + tuple(others)):
        source = lax.rem(group + groups - shift, groups)
        columns = pl.ds(pl.multiple_of(source * width, width), width)
        out_ref[0, :, columns] = dot(readout[...], part[...]).astype(BF16)


def params():
    return pltpu.CompilerParams(vmem_limit_bytes=VMEM_LIMIT)


def cost(us):
    return pl.CostEstimate(flops=int(us * 1.1e9), bytes_accessed=int(us * 1e6), transcendentals=0)


def whole(shape):
    return pl.BlockSpec(shape, lambda *a: (0,) * len(shape))


def shards(mesh, queries, keys, values, gates, ridge, out_weight):
    tokens, width = queries.shape
    heads = width // HD
    half = heads // 2
    blocks = tokens // SPAN
    seq, groups = mesh.shape["seq"], mesh.shape["head"]
    columns = out_weight.shape[1]
    side = 4
    place = lax.axis_index("seq")
    core = lax.rem(place, 2)
    x_at = lax.rem(place // 2, side)
    y_at = place // (2 * side)
    group = lax.axis_index("head")
    core_arg = core.reshape(1).astype(jnp.int32)
    group_arg = group.reshape(1).astype(jnp.int32)
    smem = pl.BlockSpec(memory_space=pltpu.SMEM)

    def perm_core():
        return [(p, p ^ 1) for p in range(seq)]

    def perm_x(shift):
        return [(p, (p // 8) * 8 + ((p // 2 + shift) % side) * 2 + p % 2) for p in range(seq)]

    def perm_y(shift):
        return [(p, (p + 8 * shift) % seq) for p in range(seq)]

    def send(array, perm):
        return lax.ppermute(array, "seq", perm)

    parts = []
    for shift in range(1, groups):
        to = lax.rem(group + shift, groups)
        piece = lax.dynamic_slice_in_dim(out_weight, to * width, width, 0)
        parts.append(
            lax.ppermute(piece, "head", [(i, (i + shift) % groups) for i in range(groups)])
        )

    square = (half, HD, HD)
    by_head = pl.BlockSpec((tokens, HD), lambda h: (0, h))
    head_turned = pl.BlockSpec((1, HD, tokens), lambda h: (h, 0, 0))
    head_blocks = pl.BlockSpec((1, blocks, HD, HD), lambda h: (h, 0, 0, 0))
    turned_shape = jax.ShapeDtypeStruct((heads, HD, tokens), BF16)
    block_shape = jax.ShapeDtypeStruct((heads, blocks, HD, HD), F32)
    row = pl.BlockSpec((1, 1, tokens), lambda h: (h, 0, 0))
    row_shape = jax.ShapeDtypeStruct((heads, 1, tokens), F32)
    mine, theirs, keys_turned, scale, gated = pl.pallas_call(
        functools.partial(totals_kernel, half),
        grid=(heads,),
        in_specs=[smem, by_head, whole((heads, tokens))],
        out_specs=[whole(square), whole(square), head_turned, row, row],
        out_shape=[jax.ShapeDtypeStruct(square, F32)] * 2
        + [turned_shape, row_shape, row_shape],
        compiler_params=params(),
        cost_estimate=cost(3),
        name="totals",
    )(core_arg, keys, gates.T)

    moment_total = pl.pallas_call(
        moment_kernel,
        grid=(heads,),
        in_specs=[head_turned, row, by_head],
        out_specs=pl.BlockSpec((1, HD, HD), lambda h: (h, 0, 0)),
        out_shape=jax.ShapeDtypeStruct((heads, HD, HD), BF16),
        compiler_params=params(),
        cost_estimate=cost(3),
        name="moments",
    )(keys_turned, gated, values)

    def before_of(parts, at):
        return sum(jnp.where(at >= shift, part.astype(F32), 0.0) for shift, part in enumerate(parts, 1))

    def total_of(own, parts):
        return (own.astype(F32) + sum(part.astype(F32) for part in parts)).astype(own.dtype)

    received = send(theirs, perm_core())
    other = send(moment_total, perm_core())
    chip = (mine + received).astype(F16)
    chip, keys_turned_later = lax.optimization_barrier((chip, keys_turned))
    along = [send(chip, perm_x(shift)) for shift in range(1, side)]
    local_gram, local_moment, values_turned = pl.pallas_call(
        functools.partial(local_kernel, blocks),
        grid=(heads,),
        in_specs=[head_turned, row, row, by_head, by_head],
        out_specs=[head_blocks, head_blocks, head_turned],
        out_shape=[block_shape, block_shape, turned_shape],
        compiler_params=params(),
        cost_estimate=cost(5),
        name="local",
    )(keys_turned_later, scale, gated, keys, values)

    row_total = total_of(chip, along)
    moment_chip = (moment_total.astype(F32) + other.astype(F32)).astype(BF16)
    row_total, moment_chip, queries_later = lax.optimization_barrier((row_total, moment_chip, queries))
    above = [send(row_total, perm_y(shift)) for shift in range(1, side)]
    moment_along = [send(moment_chip, perm_x(shift)) for shift in range(1, side)]
    queries_turned, gram_mask, moment_mask = pl.pallas_call(
        functools.partial(masks_kernel, blocks),
        grid=(heads,),
        in_specs=[by_head, row, row],
        out_specs=[head_turned, head_blocks, head_blocks],
        out_shape=[turned_shape, block_shape, block_shape],
        compiler_params=params(),
        cost_estimate=cost(4),
        name="masks",
    )(queries_later, scale, gated)

    before = before_of(along, x_at) + before_of(above, y_at)
    keep = before + jnp.where(core == 1, received, 0.0)
    give = before + jnp.where(core == 0, mine, 0.0)
    got = send(give, perm_core())
    moment_row = total_of(moment_chip, moment_along)
    keep, got, moment_row, parts = lax.optimization_barrier((keep, got, moment_row, parts))
    moment_above = [send(moment_row, perm_y(shift)) for shift in range(1, side)]
    moment_before = before_of(moment_along, x_at) + jnp.where(core == 1, other, jnp.zeros_like(other)).astype(F32)

    step_blocks = 4
    step = step_blocks * SPAN
    units = heads * step_blocks
    tall = pl.BlockSpec((heads, HD, step), lambda b: (0, 0, b))
    some_blocks = pl.BlockSpec((heads, step_blocks, HD, HD), lambda b: (0, b, 0, 0))
    high, low, corr = pl.pallas_call(
        functools.partial(solve_kernel, heads, step_blocks),
        grid=(blocks // step_blocks,),
        in_specs=[
            smem,
            smem,
            tall,
            pl.BlockSpec((step, width), lambda b: (b, 0)),
            tall,
            some_blocks,
            some_blocks,
            some_blocks,
            whole(square),
            whole(square),
        ],
        out_specs=[tall] * 3,
        out_shape=[turned_shape] * 3,
        scratch_shapes=[
            pltpu.VMEM((units, 2 * HD, 2 * HD), BF16),
            pltpu.VMEM((units, HD, 2 * HD), BF16),
            pltpu.VMEM((units, HD, SPAN), F32),
            pltpu.VMEM((units, HD, SPAN), F32),
            pltpu.VMEM((units, HD, SPAN), F32),
            pltpu.VMEM((units, 1, SPAN), F32),
        ],
        compiler_params=params(),
        cost_estimate=cost(30),
        name="solve",
    )(core_arg, ridge, queries_turned, keys, keys_turned, gram_mask, moment_mask, local_gram, keep, got)

    moment_prior = moment_before + before_of(moment_above, y_at)
    out_blocks = 2
    step = out_blocks * SPAN
    tall = pl.BlockSpec((heads, HD, step), lambda b, g: (0, 0, b))
    out = pl.pallas_call(
        functools.partial(project_kernel, heads, out_blocks, groups),
        grid_spec=pltpu.PrefetchScalarGridSpec(
            num_scalar_prefetch=1,
            grid=(blocks // out_blocks,),
            in_specs=[
                tall,
                tall,
                tall,
                tall,
                pl.BlockSpec((heads, out_blocks, HD, HD), lambda b, g: (0, b, 0, 0)),
                whole((heads, HD, HD)),
                pl.BlockSpec((width, columns), lambda b, g: (g[0], 0)),
            ]
            + [whole((width, columns))] * (groups - 1),
            out_specs=pl.BlockSpec((1, step, columns * groups), lambda b, g: (0, b, 0)),
            scratch_shapes=[pltpu.VMEM((step, width), BF16)],
        ),
        out_shape=jax.ShapeDtypeStruct((1, tokens, columns * groups), BF16),
        compiler_params=params(),
        cost_estimate=cost(7),
        name="project",
    )(group_arg, values_turned, high, low, corr, local_moment, moment_prior, out_weight, *parts)
    return out


def solution(mesh):
    return jax.shard_map(
        functools.partial(shards, mesh),
        mesh=mesh,
        in_specs=(
            P("seq", "head"),
            P("seq", "head"),
            P("seq", "head"),
            P("seq", "head"),
            P("head"),
            P(None, "head"),
        ),
        out_specs=P("head", "seq", None),
        check_vma=False,
    )
```

```python
import functools
import jax
import jax.numpy as jnp
from jax import lax
from jax.experimental import pallas as pl
from jax.experimental.pallas import tpu as pltpu
from jax.sharding import PartitionSpec as P

HD = 128
SPAN = 128
ITERS = 8
EPS = 1e-06
F32 = jnp.float32
BF16 = jnp.bfloat16
F16 = jnp.float16
SHRINK = 16.0
VMEM_LIMIT = 56 * 1024 * 1024


def two_terms(value):
    high = value.astype(BF16)
    return high, (value - high.astype(F32)).astype(BF16)


def dot(left, right):
    return jnp.dot(left, right, preferred_element_type=F32)


def head_cols(head):
    return slice(head * HD, (head + 1) * HD)


def totals_kernel(
    half, core_ref, keys_ref, values_ref, gates_ref, mine_ref, theirs_ref, turned_ref, scale_ref, gated_ref
):
    step = pl.program_id(0)
    gates = gates_ref[pl.ds(step, 1)][0]
    lefts = []
    for head in range(half):
        turned = keys_ref[:, head_cols(head)].T
        turned_ref[head] = turned
        wide = turned.astype(F32)
        norm = jnp.sum(wide * wide, axis=0, keepdims=True) + EPS
        gate = gates[head : head + 1]
        scale = gate / norm
        gated = gate * lax.rsqrt(norm)
        scale_ref[head] = scale
        gated_ref[head] = gated
        for factor in (scale, gated * (1.0 / SHRINK)):
            lefts.append(jnp.concatenate(two_terms(wide * factor), axis=0))
    grams = [dot(lefts[2 * head], keys_ref[:, head_cols(head)]) for head in range(half)]
    moments = [dot(lefts[2 * head + 1], values_ref[:, head_cols(head)]) for head in range(half)]
    sums = [product[:HD] + product[HD:] for product in grams + moments]
    own = core_ref[0] == step

    @pl.when(own)
    def _():
        for at, value in enumerate(sums):
            mine_ref[at] = value

    @pl.when(jnp.logical_not(own))
    def _():
        for at, value in enumerate(sums):
            theirs_ref[at] = value


def local_kernel(blocks, turned_ref, scale_ref, gated_ref, keys_ref, values_ref, gram_ref, moment_ref, values_turned_ref):
    values_turned_ref[0] = values_ref[...].T
    gram_ref[0, 0] = jnp.zeros((HD, HD), F32)
    moment_ref[0, 0] = jnp.zeros((HD, HD), F32)
    for block in range(blocks - 1):
        span = slice(block * SPAN, (block + 1) * SPAN)
        keys = turned_ref[0, :, span].astype(F32)
        high, low = two_terms(keys * scale_ref[0, :, span])
        product = dot(jnp.concatenate([high, low], axis=0), keys_ref[span, :])
        gram_ref[0, block + 1] = gram_ref[0, block] + (product[:HD] + product[HD:])
        high, low = two_terms(keys * gated_ref[0, :, span])
        product = dot(jnp.concatenate([high, low], axis=0), values_ref[span, :])
        moment_ref[0, block + 1] = moment_ref[0, block] + (product[:HD] + product[HD:]).T


def masks_kernel(blocks, queries_ref, scale_ref, gated_ref, turned_ref, gram_mask_ref, moment_mask_ref):
    row = lax.broadcasted_iota(jnp.int32, (SPAN, SPAN), 0)
    column = lax.broadcasted_iota(jnp.int32, (SPAN, SPAN), 1)
    turned_ref[0] = queries_ref[...].T
    for block in range(blocks):
        span = slice(block * SPAN, (block + 1) * SPAN)
        for out_ref, factors in ((gram_mask_ref, scale_ref), (moment_mask_ref, gated_ref)):
            factor = jnp.broadcast_to(factors[0, :, span], (SPAN, SPAN)).T
            out_ref[0, block] = jnp.where(row <= column, factor, 0.0)


def solve_kernel(
    heads,
    blocks,
    core_ref,
    ridge_ref,
    queries_ref,
    keys_ref,
    turned_ref,
    gram_mask_ref,
    moment_mask_ref,
    local_ref,
    keep_ref,
    got_ref,
    high_ref,
    low_ref,
    corr_ref,
    first,
    second,
    xs,
    rs,
    ds,
    norms,
):
    core = core_ref[0]
    half = heads // 2
    row = lax.broadcasted_iota(jnp.int32, (SPAN, SPAN), 0)
    column = lax.broadcasted_iota(jnp.int32, (SPAN, SPAN), 1)
    units = [(head, block) for block in range(blocks) for head in range(heads)]
    count = len(units)
    for head in range(heads):
        prior = jnp.where(core == head // half, keep_ref[head % half], got_ref[head % half])
        prior = prior + jnp.where(row == column, ridge_ref[head], 0.0)
        for block in range(blocks):
            unit = block * heads + head
            rows = slice(block * SPAN, (block + 1) * SPAN)
            own = keys_ref[rows, head_cols(head)]
            high, low = two_terms(prior + local_ref[head, block])
            first[unit, :HD, :HD] = high
            first[unit, :HD, HD:] = high
            first[unit, HD:, :HD] = own
            first[unit, HD:, HD:] = own
            second[unit, :, :HD] = low
            second[unit, :, HD:] = turned_ref[head, :, rows]
            query = queries_ref[head, :, rows].astype(F32)
            query = query * lax.rsqrt(jnp.sum(query * query, axis=0, keepdims=True) + EPS)
            xs[unit] = jnp.zeros((HD, SPAN), F32)
            rs[unit] = query
            ds[unit] = query
            norms[unit] = jnp.sum(query * query, axis=0, keepdims=True)

    def product_of(unit):
        high, low = two_terms(ds[unit])
        return high, dot(first[unit], jnp.concatenate([high, low], axis=0))

    def image_of(unit, high, product):
        head, block = units[unit]
        corr = (product[HD:] * gram_mask_ref[head, block]).astype(BF16)
        return product[:HD] + dot(second[unit], jnp.concatenate([high, corr], axis=0))

    def update(unit, image):
        direction = ds[unit]
        now = norms[unit]
        step = now / (jnp.sum(direction * image, axis=0, keepdims=True) + EPS)
        xs[unit] += step * direction
        residual = rs[unit] - step * image
        rs[unit] = residual
        after = jnp.sum(residual * residual, axis=0, keepdims=True)
        ds[unit] = residual + (after / (now + EPS)) * direction
        norms[unit] = after

    lag = 4

    def sweep_once(sweep, carry):
        products, images = {}, {}
        for at in range(count + 2 * lag):
            if at < count:
                products[at] = product_of(at)
            if 0 <= at - lag < count:
                images[at - lag] = image_of(at - lag, *products.pop(at - lag))
            if 0 <= at - 2 * lag < count:
                update(at - 2 * lag, images.pop(at - 2 * lag))
        return carry

    lax.fori_loop(0, ITERS, sweep_once, 0)
    for unit, (head, block) in enumerate(units):
        rows = slice(block * SPAN, (block + 1) * SPAN)
        high, low = two_terms(xs[unit])
        corr = dot(first[unit, HD:], jnp.concatenate([high, low], axis=0))
        high_ref[head, :, rows] = high
        low_ref[head, :, rows] = low
        corr_ref[head, :, rows] = (corr * moment_mask_ref[head, block]).astype(BF16)


def project_kernel(
    heads,
    blocks,
    groups,
    place_ref,
    values_ref,
    high_ref,
    low_ref,
    corr_ref,
    local_ref,
    keep_ref,
    got_ref,
    own_ref,
    *rest,
):
    others, out_ref = rest[: groups - 1], rest[groups - 1]
    readout, prior = rest[groups], rest[groups + 1]
    half = heads // 2

    @pl.when(pl.program_id(0) == 0)
    def _():
        for head in range(heads):
            at = half + head % half
            prior[head] = jnp.where(place_ref[1] == head // half, keep_ref[at], got_ref[at]).T * SHRINK

    units = [(head, slice(block * SPAN, (block + 1) * SPAN), block) for head in range(heads) for block in range(blocks)]
    products = []
    for head, rows, block in units:
        moment_high, moment_low = two_terms(prior[head] + local_ref[head, block])
        left = jnp.concatenate([moment_high, moment_high, moment_low, values_ref[head, :, rows]], axis=1)
        high = high_ref[head, :, rows]
        right = jnp.concatenate([high, low_ref[head, :, rows], high, corr_ref[head, :, rows]], axis=0)
        products.append(dot(left, right))
    for (head, rows, block), product in zip(units, products):
        readout[rows, head_cols(head)] = product.T.astype(BF16)
    group = place_ref[0]
    width = own_ref.shape[1]
    for shift, part in enumerate((own_ref,) + tuple(others)):
        source = lax.rem(group + groups - shift, groups)
        columns = pl.ds(pl.multiple_of(source * width, width), width)
        out_ref[0, :, columns] = dot(readout[...], part[...]).astype(BF16)


def params():
    return pltpu.CompilerParams(vmem_limit_bytes=VMEM_LIMIT)


def cost(us):
    return pl.CostEstimate(flops=int(us * 1.1e9), bytes_accessed=int(us * 1e6), transcendentals=0)


def whole(shape):
    return pl.BlockSpec(shape, lambda *a: (0,) * len(shape))


def shards(mesh, queries, keys, values, gates, ridge, out_weight):
    tokens, width = queries.shape
    heads = width // HD
    half = heads // 2
    blocks = tokens // SPAN
    seq, groups = mesh.shape["seq"], mesh.shape["head"]
    columns = out_weight.shape[1]
    side = 4
    place = lax.axis_index("seq")
    core = lax.rem(place, 2)
    x_at = lax.rem(place // 2, side)
    y_at = place // (2 * side)
    group = lax.axis_index("head")
    core_arg = core.reshape(1).astype(jnp.int32)
    place_arg = jnp.stack([group, core]).astype(jnp.int32)
    smem = pl.BlockSpec(memory_space=pltpu.SMEM)

    def perm_core():
        return [(p, p ^ 1) for p in range(seq)]

    def perm_x(shift):
        return [(p, (p // 8) * 8 + ((p // 2 + shift) % side) * 2 + p % 2) for p in range(seq)]

    def perm_y(shift):
        return [(p, (p + 8 * shift) % seq) for p in range(seq)]

    def send(array, perm):
        return lax.ppermute(array, "seq", perm)

    def rows_from(shift, weight):
        piece = lax.dynamic_slice_in_dim(weight, lax.rem(group + shift, groups) * width, width, 0)
        return lax.ppermute(piece, "head", [(i, (i + shift) % groups) for i in range(groups)])

    sums = (2 * half, HD, HD)
    by_head = pl.BlockSpec((tokens, HD), lambda h: (0, h))
    head_turned = pl.BlockSpec((1, HD, tokens), lambda h: (h, 0, 0))
    head_blocks = pl.BlockSpec((1, blocks, HD, HD), lambda h: (h, 0, 0, 0))
    row = pl.BlockSpec((1, 1, tokens), lambda h: (h, 0, 0))
    row_shape = jax.ShapeDtypeStruct((heads, 1, tokens), F32)
    turned_shape = jax.ShapeDtypeStruct((heads, HD, tokens), BF16)
    block_shape = jax.ShapeDtypeStruct((heads, blocks, HD, HD), F32)
    by_half = pl.BlockSpec((tokens, half * HD), lambda s: (0, s))
    half_row = pl.BlockSpec((half, 1, tokens), lambda s: (s, 0, 0))
    mine, theirs, keys_turned, scale, gated = pl.pallas_call(
        functools.partial(totals_kernel, half),
        grid=(2,),
        in_specs=[smem, by_half, by_half, whole((2, half, tokens))],
        out_specs=[
            whole(sums),
            whole(sums),
            pl.BlockSpec((half, HD, tokens), lambda s: (s, 0, 0)),
            half_row,
            half_row,
        ],
        out_shape=[jax.ShapeDtypeStruct(sums, F32)] * 2 + [turned_shape, row_shape, row_shape],
        compiler_params=params(),
        cost_estimate=cost(5),
        name="totals",
    )(core_arg, keys, values, gates.T.reshape(2, half, tokens))

    def before_of(parts, at):
        return sum(jnp.where(at >= shift, part.astype(F32), 0.0) for shift, part in enumerate(parts, 1))

    received = send(theirs, perm_core())
    chip = (mine + received).astype(F16)
    chip, keys_turned_later, weight = lax.optimization_barrier((chip, keys_turned, out_weight))
    along = [send(chip, perm_x(shift)) for shift in range(1, side)]
    parts = [rows_from(shift, weight) for shift in range(1, groups - 1)]
    local_gram, local_moment, values_turned = pl.pallas_call(
        functools.partial(local_kernel, blocks),
        grid=(heads,),
        in_specs=[head_turned, row, row, by_head, by_head],
        out_specs=[head_blocks, head_blocks, head_turned],
        out_shape=[block_shape, block_shape, turned_shape],
        compiler_params=params(),
        cost_estimate=cost(5),
        name="local",
    )(keys_turned_later, scale, gated, keys, values)

    row_total = (chip.astype(F32) + sum(part.astype(F32) for part in along)).astype(F16)
    row_total, queries_later = lax.optimization_barrier((row_total, queries))
    above = [send(row_total, perm_y(shift)) for shift in range(1, side)]
    queries_turned, gram_mask, moment_mask = pl.pallas_call(
        functools.partial(masks_kernel, blocks),
        grid=(heads,),
        in_specs=[by_head, row, row],
        out_specs=[head_turned, head_blocks, head_blocks],
        out_shape=[turned_shape, block_shape, block_shape],
        compiler_params=params(),
        cost_estimate=cost(4),
        name="masks",
    )(queries_later, scale, gated)

    above, weight = lax.optimization_barrier((above, weight))
    parts.append(rows_from(groups - 1, weight))
    before = before_of(along, x_at) + before_of(above, y_at)
    keep = before + jnp.where(core == 1, received, 0.0)
    give = before + jnp.where(core == 0, mine, 0.0)
    got = send(give, perm_core())

    step_blocks = 4
    step = step_blocks * SPAN
    units = heads * step_blocks
    tall = pl.BlockSpec((heads, HD, step), lambda b: (0, 0, b))
    some_blocks = pl.BlockSpec((heads, step_blocks, HD, HD), lambda b: (0, b, 0, 0))
    high, low, corr = pl.pallas_call(
        functools.partial(solve_kernel, heads, step_blocks),
        grid=(blocks // step_blocks,),
        in_specs=[
            smem,
            smem,
            tall,
            pl.BlockSpec((step, width), lambda b: (b, 0)),
            tall,
            some_blocks,
            some_blocks,
            some_blocks,
            whole(sums),
            whole(sums),
        ],
        out_specs=[tall] * 3,
        out_shape=[turned_shape] * 3,
        scratch_shapes=[
            pltpu.VMEM((units, 2 * HD, 2 * HD), BF16),
            pltpu.VMEM((units, HD, 2 * HD), BF16),
            pltpu.VMEM((units, HD, SPAN), F32),
            pltpu.VMEM((units, HD, SPAN), F32),
            pltpu.VMEM((units, HD, SPAN), F32),
            pltpu.VMEM((units, 1, SPAN), F32),
        ],
        compiler_params=params(),
        cost_estimate=cost(30),
        name="solve",
    )(core_arg, ridge, queries_turned, keys, keys_turned, gram_mask, moment_mask, local_gram, keep, got)

    out_blocks = 2
    step = out_blocks * SPAN
    tall = pl.BlockSpec((heads, HD, step), lambda b, g: (0, 0, b))
    out = pl.pallas_call(
        functools.partial(project_kernel, heads, out_blocks, groups),
        grid_spec=pltpu.PrefetchScalarGridSpec(
            num_scalar_prefetch=1,
            grid=(blocks // out_blocks,),
            in_specs=[
                tall,
                tall,
                tall,
                tall,
                pl.BlockSpec((heads, out_blocks, HD, HD), lambda b, g: (0, b, 0, 0)),
                whole(sums),
                whole(sums),
                pl.BlockSpec((width, columns), lambda b, g: (g[0], 0)),
            ]
            + [whole((width, columns))] * (groups - 1),
            out_specs=pl.BlockSpec((1, step, columns * groups), lambda b, g: (0, b, 0)),
            scratch_shapes=[pltpu.VMEM((step, width), BF16), pltpu.VMEM((heads, HD, HD), F32)],
        ),
        out_shape=jax.ShapeDtypeStruct((1, tokens, columns * groups), BF16),
        compiler_params=params(),
        cost_estimate=cost(7),
        name="project",
    )(place_arg, values_turned, high, low, corr, local_moment, keep, got, out_weight, *parts)
    return out


def solution(mesh):
    return jax.shard_map(
        functools.partial(shards, mesh),
        mesh=mesh,
        in_specs=(
            P("seq", "head"),
            P("seq", "head"),
            P("seq", "head"),
            P("seq", "head"),
            P("head"),
            P(None, "head"),
        ),
        out_specs=P("head", "seq", None),
        check_vma=False,
    )
```

```python
import functools
import jax
import jax.numpy as jnp
from jax import lax
from jax.experimental import pallas as pl
from jax.experimental.pallas import tpu as pltpu
from jax.sharding import PartitionSpec as P

HD = 128
SPAN = 128
ITERS = 8
EPS = 1e-06
F32 = jnp.float32
BF16 = jnp.bfloat16
F16 = jnp.float16
SHRINK = 16.0


def two_terms(value):
    high = value.astype(BF16)
    return high, (value - high.astype(F32)).astype(BF16)


def dot(left, right):
    return jnp.dot(left, right, preferred_element_type=F32)


def head_cols(head):
    return slice(head * HD, (head + 1) * HD)


def totals_kernel(
    half, core_ref, keys_ref, values_ref, gates_ref, mine_ref, theirs_ref, turned_ref, scale_ref, gated_ref
):
    step = pl.program_id(0)
    lefts = []
    for head in range(half):
        turned = keys_ref[:, head_cols(head)].T
        turned_ref[head] = turned
        wide = turned.astype(F32)
        norm = jnp.sum(wide * wide, axis=0, keepdims=True) + EPS
        gate = gates_ref[pl.ds(step * half + head, 1), :]
        scale = gate / norm
        gated = gate * lax.rsqrt(norm)
        scale_ref[head] = scale
        gated_ref[head] = gated
        for factor in (scale, gated * (1.0 / SHRINK)):
            lefts.append(jnp.concatenate(two_terms(wide * factor), axis=0))
    grams = [dot(lefts[2 * head], keys_ref[:, head_cols(head)]) for head in range(half)]
    moments = [dot(lefts[2 * head + 1], values_ref[:, head_cols(head)]) for head in range(half)]
    sums = [product[:HD] + product[HD:] for product in grams + moments]
    own = core_ref[0] == step

    @pl.when(own)
    def _():
        for at, value in enumerate(sums):
            mine_ref[at] = value

    @pl.when(jnp.logical_not(own))
    def _():
        for at, value in enumerate(sums):
            theirs_ref[at] = value


def local_kernel(blocks, turned_ref, scale_ref, gated_ref, keys_ref, values_ref, gram_ref, moment_ref, values_turned_ref):
    values_turned_ref[0] = values_ref[...].T
    gram_ref[0, 0] = jnp.zeros((HD, HD), F32)
    moment_ref[0, 0] = jnp.zeros((HD, HD), F32)
    grams, moments = [], []
    for block in range(blocks - 1):
        span = slice(block * SPAN, (block + 1) * SPAN)
        keys = turned_ref[0, :, span].astype(F32)
        left = jnp.concatenate(two_terms(keys * scale_ref[0, :, span]), axis=0)
        grams.append(dot(left, keys_ref[span, :]))
        left = jnp.concatenate(two_terms(keys * gated_ref[0, :, span]), axis=0)
        moments.append(dot(left, values_ref[span, :]))
    for block in range(blocks - 1):
        gram, moment = grams[block], moments[block]
        gram_ref[0, block + 1] = gram_ref[0, block] + (gram[:HD] + gram[HD:])
        moment_ref[0, block + 1] = moment_ref[0, block] + (moment[:HD] + moment[HD:]).T


def columns_kernel(blocks, queries_ref, scale_ref, gated_ref, turned_ref, scale_out_ref, gated_out_ref):
    turned_ref[0] = queries_ref[...].T
    for out_ref, factors in ((scale_out_ref, scale_ref), (gated_out_ref, gated_ref)):
        spans = [factors[0, :, block * SPAN : (block + 1) * SPAN] for block in range(blocks)]
        spans += [jnp.zeros((1, SPAN), F32)] * (SPAN - blocks)
        out_ref[0] = jnp.concatenate(spans, axis=0).T


def solve_kernel(
    heads,
    blocks,
    steps,
    core_ref,
    ridge_ref,
    queries_ref,
    keys_ref,
    turned_ref,
    scale_ref,
    gated_ref,
    local_ref,
    values_ref,
    local_moment_ref,
    keep_ref,
    got_ref,
    readout_ref,
    first,
    second,
    masks,
    xs,
    rs,
    ds,
    norms,
):
    core = core_ref[0]
    half = heads // 2
    row = lax.broadcasted_iota(jnp.int32, (SPAN, SPAN), 0)
    column = lax.broadcasted_iota(jnp.int32, (SPAN, SPAN), 1)
    causal = row <= column
    units = [(head, block) for block in range(blocks) for head in range(heads)]
    count = len(units)
    step = pl.program_id(0)

    def column_of(ref, head, block):
        options = [ref[head, :, at * blocks + block : at * blocks + block + 1] for at in range(steps)]
        value = options[0]
        for at in range(1, steps):
            value = jnp.where(step == at, options[at], value)
        return value

    for head in range(heads):
        prior = jnp.where(core == head // half, keep_ref[head % half], got_ref[head % half])
        prior = prior + jnp.where(row == column, ridge_ref[head], 0.0)
        for block in range(blocks):
            unit = block * heads + head
            rows = slice(block * SPAN, (block + 1) * SPAN)
            own = keys_ref[rows, head_cols(head)]
            masks[unit] = jnp.where(causal, column_of(scale_ref, head, block), 0.0)
            high, low = two_terms(prior + local_ref[head, block])
            first[unit, :HD, :HD] = high
            first[unit, :HD, HD:] = high
            first[unit, HD:, :HD] = own
            first[unit, HD:, HD:] = own
            second[unit, :, :HD] = low
            second[unit, :, HD:] = turned_ref[head, :, rows]
            query = queries_ref[head, :, rows].astype(F32)
            query = query * lax.rsqrt(jnp.sum(query * query, axis=0, keepdims=True) + EPS)
            xs[unit] = jnp.zeros((HD, SPAN), F32)
            rs[unit] = query
            ds[unit] = query
            norms[unit] = jnp.sum(query * query, axis=0, keepdims=True)

    def product_of(unit):
        high, low = two_terms(ds[unit])
        return high, dot(first[unit], jnp.concatenate([high, low], axis=0))

    def image_of(unit, high, product):
        corr = (product[HD:] * masks[unit]).astype(BF16)
        return product[:HD] + dot(second[unit], jnp.concatenate([high, corr], axis=0))

    def update(unit, image):
        direction = ds[unit]
        now = norms[unit]
        step = now / (jnp.sum(direction * image, axis=0, keepdims=True) + EPS)
        xs[unit] += step * direction
        residual = rs[unit] - step * image
        rs[unit] = residual
        after = jnp.sum(residual * residual, axis=0, keepdims=True)
        ds[unit] = residual + (after / (now + EPS)) * direction
        norms[unit] = after

    lag = 4

    def sweep_once(sweep, carry):
        products, images = {}, {}
        for at in range(count + 2 * lag):
            if at < count:
                products[at] = product_of(at)
            if 0 <= at - lag < count:
                images[at - lag] = image_of(at - lag, *products.pop(at - lag))
            if 0 <= at - 2 * lag < count:
                update(at - 2 * lag, images.pop(at - 2 * lag))
        return carry

    lax.fori_loop(0, ITERS, sweep_once, 0)

    priors = []
    for head in range(heads):
        at = half + head % half
        priors.append(jnp.where(core == head // half, keep_ref[at], got_ref[at]).T * SHRINK)

    def correlations_of(unit):
        high, low = two_terms(xs[unit])
        return high, low, dot(first[unit, HD:], jnp.concatenate([high, low], axis=0))

    def readout_of(unit, high, low, product):
        head, block = units[unit]
        corr = jnp.where(causal, product * column_of(gated_ref, head, block), 0.0).astype(BF16)
        moment_high, moment_low = two_terms(priors[head] + local_moment_ref[head, block])
        values = values_ref[head, :, block * SPAN : (block + 1) * SPAN]
        left = jnp.concatenate([moment_high, moment_high, moment_low, values], axis=1)
        return dot(left, jnp.concatenate([high, low, high, corr], axis=0))

    products, readouts = {}, {}
    for at in range(count + 2 * lag):
        if at < count:
            products[at] = correlations_of(at)
        if 0 <= at - lag < count:
            readouts[at - lag] = readout_of(at - lag, *products.pop(at - lag))
        if 0 <= at - 2 * lag < count:
            head, block = units[at - 2 * lag]
            rows = slice(block * SPAN, (block + 1) * SPAN)
            readout_ref[rows, head_cols(head)] = readouts.pop(at - 2 * lag).T.astype(BF16)


def project_kernel(groups, group_ref, readout_ref, own_ref, *rest):
    others, out_ref = rest[: groups - 1], rest[groups - 1]
    group = group_ref[0]
    width = own_ref.shape[1]
    for shift, part in enumerate((own_ref,) + tuple(others)):
        source = lax.rem(group + groups - shift, groups)
        columns = pl.ds(pl.multiple_of(source * width, width), width)
        out_ref[0, :, columns] = dot(readout_ref[...], part[...]).astype(BF16)


def params(mebibytes):
    return pltpu.CompilerParams(vmem_limit_bytes=mebibytes << 20)


def cost(us):
    return pl.CostEstimate(flops=int(us * 1.1e9), bytes_accessed=int(us * 1e6), transcendentals=0)


def whole(shape):
    return pl.BlockSpec(shape, lambda *a: (0,) * len(shape))


def shards(mesh, queries, keys, values, gates, ridge, out_weight):
    tokens, width = queries.shape
    heads = width // HD
    half = heads // 2
    blocks = tokens // SPAN
    seq, groups = mesh.shape["seq"], mesh.shape["head"]
    columns = out_weight.shape[1]
    side = 4
    place = lax.axis_index("seq")
    core = lax.rem(place, 2)
    x_at = lax.rem(place // 2, side)
    y_at = place // (2 * side)
    group = lax.axis_index("head")
    core_arg = core.reshape(1).astype(jnp.int32)
    group_arg = group.reshape(1).astype(jnp.int32)
    smem = pl.BlockSpec(memory_space=pltpu.SMEM)

    def perm_core():
        return [(p, p ^ 1) for p in range(seq)]

    def perm_x(shift):
        return [(p, (p // 8) * 8 + ((p // 2 + shift) % side) * 2 + p % 2) for p in range(seq)]

    def perm_y(shift):
        return [(p, (p + 8 * shift) % seq) for p in range(seq)]

    def send(array, perm):
        return lax.ppermute(array, "seq", perm)

    def rows_from(shift, weight):
        piece = lax.dynamic_slice_in_dim(weight, lax.rem(group + shift, groups) * width, width, 0)
        return lax.ppermute(piece, "head", [(i, (i + shift) % groups) for i in range(groups)])

    sums = (2 * half, HD, HD)
    by_head = pl.BlockSpec((tokens, HD), lambda h: (0, h))
    head_turned = pl.BlockSpec((1, HD, tokens), lambda h: (h, 0, 0))
    head_blocks = pl.BlockSpec((1, blocks, HD, HD), lambda h: (h, 0, 0, 0))
    row = pl.BlockSpec((1, 1, tokens), lambda h: (h, 0, 0))
    row_shape = jax.ShapeDtypeStruct((heads, 1, tokens), F32)
    turned_shape = jax.ShapeDtypeStruct((heads, HD, tokens), BF16)
    block_shape = jax.ShapeDtypeStruct((heads, blocks, HD, HD), F32)
    by_half = pl.BlockSpec((tokens, half * HD), lambda s: (0, s))
    half_row = pl.BlockSpec((half, 1, tokens), lambda s: (s, 0, 0))
    mine, theirs, keys_turned, scale, gated = pl.pallas_call(
        functools.partial(totals_kernel, half),
        grid=(2,),
        in_specs=[smem, by_half, by_half, whole((heads, tokens))],
        out_specs=[
            whole(sums),
            whole(sums),
            pl.BlockSpec((half, HD, tokens), lambda s: (s, 0, 0)),
            half_row,
            half_row,
        ],
        out_shape=[jax.ShapeDtypeStruct(sums, F32)] * 2 + [turned_shape, row_shape, row_shape],
        compiler_params=params(60),
        cost_estimate=cost(5),
        name="totals",
    )(core_arg, keys, values, gates.T)

    def before_of(parts, at):
        return sum(jnp.where(at >= shift, part.astype(F32), 0.0) for shift, part in enumerate(parts, 1))

    received = send(theirs, perm_core())
    chip = (mine + received).astype(F16)
    chip, keys_turned_later, weight = lax.optimization_barrier((chip, keys_turned, out_weight))
    along = [send(chip, perm_x(shift)) for shift in range(1, side)]
    parts = [rows_from(1, weight)]
    local_gram, local_moment, values_turned = pl.pallas_call(
        functools.partial(local_kernel, blocks),
        grid=(heads,),
        in_specs=[head_turned, row, row, by_head, by_head],
        out_specs=[head_blocks, head_blocks, head_turned],
        out_shape=[block_shape, block_shape, turned_shape],
        compiler_params=params(16),
        cost_estimate=cost(5),
        name="local",
    )(keys_turned_later, scale, gated, keys, values)

    row_total = (chip.astype(F32) + sum(part.astype(F32) for part in along)).astype(F16)
    row_total, queries_later, weight = lax.optimization_barrier((row_total, queries, weight))
    above = [send(row_total, perm_y(shift)) for shift in range(1, side)]
    parts += [rows_from(shift, weight) for shift in range(2, groups - 1)]
    columns_spec = pl.BlockSpec((1, SPAN, SPAN), lambda h: (h, 0, 0))
    columns_shape = jax.ShapeDtypeStruct((heads, SPAN, SPAN), F32)
    queries_turned, scale_columns, gated_columns = pl.pallas_call(
        functools.partial(columns_kernel, blocks),
        grid=(heads,),
        in_specs=[by_head, row, row],
        out_specs=[head_turned, columns_spec, columns_spec],
        out_shape=[turned_shape, columns_shape, columns_shape],
        compiler_params=params(16),
        cost_estimate=cost(3),
        name="columns",
    )(queries_later, scale, gated)

    above, weight = lax.optimization_barrier((above, weight))
    parts.append(rows_from(groups - 1, weight))
    before = before_of(along, x_at) + before_of(above, y_at)
    keep = before + jnp.where(core == 1, received, 0.0)
    give = before + jnp.where(core == 0, mine, 0.0)
    got = send(give, perm_core())

    step_blocks = 4
    step = step_blocks * SPAN
    units = heads * step_blocks
    tall = pl.BlockSpec((heads, HD, step), lambda b: (0, 0, b))
    some_blocks = pl.BlockSpec((heads, step_blocks, HD, HD), lambda b: (0, b, 0, 0))
    readout = pl.pallas_call(
        functools.partial(solve_kernel, heads, step_blocks, blocks // step_blocks),
        grid=(blocks // step_blocks,),
        in_specs=[
            smem,
            smem,
            tall,
            pl.BlockSpec((step, width), lambda b: (b, 0)),
            tall,
            whole((heads, SPAN, SPAN)),
            whole((heads, SPAN, SPAN)),
            some_blocks,
            tall,
            some_blocks,
            whole(sums),
            whole(sums),
        ],
        out_specs=pl.BlockSpec((step, width), lambda b: (b, 0)),
        out_shape=jax.ShapeDtypeStruct((tokens, width), BF16),
        scratch_shapes=[
            pltpu.VMEM((units, 2 * HD, 2 * HD), BF16),
            pltpu.VMEM((units, HD, 2 * HD), BF16),
            pltpu.VMEM((units, SPAN, SPAN), F32),
            pltpu.VMEM((units, HD, SPAN), F32),
            pltpu.VMEM((units, HD, SPAN), F32),
            pltpu.VMEM((units, HD, SPAN), F32),
            pltpu.VMEM((units, 1, SPAN), F32),
        ],
        compiler_params=params(32),
        cost_estimate=cost(30),
        name="solve",
    )(
        core_arg,
        ridge,
        queries_turned,
        keys,
        keys_turned,
        scale_columns,
        gated_columns,
        local_gram,
        values_turned,
        local_moment,
        keep,
        got,
    )

    step = 2 * SPAN
    out = pl.pallas_call(
        functools.partial(project_kernel, groups),
        grid_spec=pltpu.PrefetchScalarGridSpec(
            num_scalar_prefetch=1,
            grid=(tokens // step,),
            in_specs=[
                pl.BlockSpec((step, width), lambda b, g: (b, 0)),
                pl.BlockSpec((width, columns), lambda b, g: (g[0], 0)),
            ]
            + [pl.BlockSpec(memory_space=pltpu.VMEM)] * (groups - 1),
            out_specs=pl.BlockSpec((1, step, columns * groups), lambda b, g: (0, b, 0)),
        ),
        out_shape=jax.ShapeDtypeStruct((1, tokens, columns * groups), BF16),
        compiler_params=params(12),
        cost_estimate=cost(5),
        name="project",
    )(group_arg, readout, out_weight, *parts)
    return out


def solution(mesh):
    return jax.shard_map(
        functools.partial(shards, mesh),
        mesh=mesh,
        in_specs=(
            P("seq", "head"),
            P("seq", "head"),
            P("seq", "head"),
            P("seq", "head"),
            P("head"),
            P(None, "head"),
        ),
        out_specs=P("head", "seq", None),
        check_vma=False,
    )
```

```python
import functools
import jax
import jax.numpy as jnp
from jax import lax
from jax.experimental import pallas as pl
from jax.experimental.pallas import tpu as pltpu
from jax.sharding import PartitionSpec as P

HD = 128
SPAN = 128
ITERS = 8
EPS = 1e-06
F32 = jnp.float32
BF16 = jnp.bfloat16
F16 = jnp.float16
SHRINK = 16.0
LAG = 4


def two_terms(value):
    high = value.astype(BF16)
    return high, (value - high.astype(F32)).astype(BF16)


def dot(left, right):
    return jnp.dot(left, right, preferred_element_type=F32)


def head_cols(head):
    return slice(head * HD, (head + 1) * HD)


def totals_kernel(
    half, core_ref, keys_ref, values_ref, gates_ref, mine_ref, theirs_ref, turned_ref, scale_ref, gated_ref
):
    step = pl.program_id(0)
    lefts = []
    for head in range(half):
        turned = keys_ref[:, head_cols(head)].T
        turned_ref[head] = turned
        wide = turned.astype(F32)
        norm = jnp.sum(wide * wide, axis=0, keepdims=True) + EPS
        gate = gates_ref[pl.ds(step * half + head, 1), :]
        scale = gate / norm
        gated = gate * lax.rsqrt(norm)
        scale_ref[head] = scale
        gated_ref[head] = gated
        for factor in (scale, gated * (1.0 / SHRINK)):
            lefts.append(jnp.concatenate(two_terms(wide * factor), axis=0))
    grams = [dot(lefts[2 * head], keys_ref[:, head_cols(head)]) for head in range(half)]
    moments = [dot(lefts[2 * head + 1], values_ref[:, head_cols(head)]) for head in range(half)]
    sums = [product[:HD] + product[HD:] for product in grams + moments]
    own = core_ref[0] == step

    @pl.when(own)
    def _():
        for at, value in enumerate(sums):
            mine_ref[at] = value

    @pl.when(jnp.logical_not(own))
    def _():
        for at, value in enumerate(sums):
            theirs_ref[at] = value


def local_kernel(blocks, turned_ref, scale_ref, gated_ref, keys_ref, values_ref, gram_ref, moment_ref, values_turned_ref):
    values_turned_ref[0] = values_ref[...].T
    gram_ref[0, 0] = jnp.zeros((HD, HD), F32)
    moment_ref[0, 0] = jnp.zeros((HD, HD), F32)
    grams, moments = [], []
    for block in range(blocks - 1):
        span = slice(block * SPAN, (block + 1) * SPAN)
        keys = turned_ref[0, :, span].astype(F32)
        left = jnp.concatenate(two_terms(keys * scale_ref[0, :, span]), axis=0)
        grams.append(dot(left, keys_ref[span, :]))
        left = jnp.concatenate(two_terms(keys * gated_ref[0, :, span]), axis=0)
        moments.append(dot(left, values_ref[span, :]))
    for block in range(blocks - 1):
        gram, moment = grams[block], moments[block]
        gram_ref[0, block + 1] = gram_ref[0, block] + (gram[:HD] + gram[HD:])
        moment_ref[0, block + 1] = moment_ref[0, block] + (moment[:HD] + moment[HD:]).T


def columns_kernel(blocks, queries_ref, scale_ref, gated_ref, turned_ref, scale_out_ref, gated_out_ref):
    turned_ref[0] = queries_ref[...].T
    for out_ref, factors in ((scale_out_ref, scale_ref), (gated_out_ref, gated_ref)):
        spans = [factors[0, :, block * SPAN : (block + 1) * SPAN] for block in range(blocks)]
        spans += [jnp.zeros((1, SPAN), F32)] * (SPAN - blocks)
        out_ref[0] = jnp.concatenate(spans, axis=0).T


def solve_kernel(
    heads,
    blocks,
    steps,
    core_ref,
    ridge_ref,
    queries_ref,
    keys_ref,
    turned_ref,
    scale_ref,
    gated_ref,
    local_ref,
    values_ref,
    local_moment_ref,
    keep_ref,
    got_ref,
    readout_ref,
    first,
    second,
    masks,
    xs,
    rs,
    ds,
    norms,
):
    core = core_ref[0]
    row = lax.broadcasted_iota(jnp.int32, (SPAN, SPAN), 0)
    column = lax.broadcasted_iota(jnp.int32, (SPAN, SPAN), 1)
    causal = row <= column
    units = [(head, block) for block in range(blocks) for head in range(heads)]
    count = len(units)
    step = pl.program_id(0)

    def column_of(ref, head, block):
        value = ref[head, :, block : block + 1]
        for at in range(1, steps):
            other = at * blocks + block
            value = jnp.where(step == at, ref[head, :, other : other + 1], value)
        return value

    start = pl.multiple_of(step * blocks * SPAN, blocks * SPAN)
    half = heads // 2
    grams, moments = [], []
    for head in range(heads):
        own, at = core == head // half, head % half
        gram = jnp.where(own, keep_ref[at], got_ref[at])
        grams.append(gram + jnp.where(row == column, ridge_ref[head], 0.0))
        moments.append(jnp.where(own, keep_ref[half + at], got_ref[half + at]).T * SHRINK)

    def prepare(unit):
        head, block = units[unit]
        rows = pl.ds(start + block * SPAN, SPAN)
        own = keys_ref[rows, head_cols(head)]
        masks[unit] = jnp.where(causal, column_of(scale_ref, head, block), 0.0)
        high, low = two_terms(grams[head] + local_ref[head, step * blocks + block])
        first[unit, :HD, :HD] = high
        first[unit, :HD, HD:] = high
        first[unit, HD:, :HD] = own
        first[unit, HD:, HD:] = own
        second[unit, :, :HD] = low
        second[unit, :, HD:] = turned_ref[head, :, rows]
        query = queries_ref[head, :, rows].astype(F32)
        query = query * lax.rsqrt(jnp.sum(query * query, axis=0, keepdims=True) + EPS)
        xs[unit] = jnp.zeros((HD, SPAN), F32)
        rs[unit] = query
        ds[unit] = query
        norms[unit] = jnp.sum(query * query, axis=0, keepdims=True)

    def product_of(unit):
        high, low = two_terms(ds[unit])
        return high, dot(first[unit], jnp.concatenate([high, low], axis=0))

    def image_of(unit, high, product):
        corr = (product[HD:] * masks[unit]).astype(BF16)
        return product[:HD] + dot(second[unit], jnp.concatenate([high, corr], axis=0))

    def update(unit, image):
        direction = ds[unit]
        now = norms[unit]
        size = now / (jnp.sum(direction * image, axis=0, keepdims=True) + EPS)
        xs[unit] += size * direction
        residual = rs[unit] - size * image
        rs[unit] = residual
        after = jnp.sum(residual * residual, axis=0, keepdims=True)
        ds[unit] = residual + (after / (now + EPS)) * direction
        norms[unit] = after

    def correlations_of(unit):
        high, low = two_terms(xs[unit])
        return high, low, dot(first[unit, HD:], jnp.concatenate([high, low], axis=0))

    def readout_of(unit, high, low, product):
        head, block = units[unit]
        corr = jnp.where(causal, product * column_of(gated_ref, head, block), 0.0).astype(BF16)
        moment_high, moment_low = two_terms(moments[head] + local_moment_ref[head, step * blocks + block])
        values = values_ref[head, :, pl.ds(start + block * SPAN, SPAN)]
        left = jnp.concatenate([moment_high, moment_high, moment_low, values], axis=1)
        return dot(left, jnp.concatenate([high, low, high, corr], axis=0))

    def store(unit, readout):
        head, block = units[unit]
        readout_ref[block * SPAN : (block + 1) * SPAN, head_cols(head)] = readout.T.astype(BF16)

    solved = ITERS * count
    products, images = {}, {}
    for at in range(solved + count + 2 * LAG):
        if at < count:
            prepare(at)
        if at < solved + count:
            products[at] = product_of(at % count) if at < solved else correlations_of(at % count)
        then = at - LAG
        if 0 <= then < solved + count:
            stage = image_of if then < solved else readout_of
            images[then] = stage(then % count, *products.pop(then))
        then = at - 2 * LAG
        if 0 <= then < solved + count:
            stage = update if then < solved else store
            stage(then % count, images.pop(then))


def project_kernel(groups, group_ref, readout_ref, own_ref, *rest):
    others, out_ref = rest[: groups - 1], rest[groups - 1]
    group = group_ref[0]
    width = own_ref.shape[1]
    for shift, part in enumerate((own_ref,) + tuple(others)):
        source = lax.rem(group + groups - shift, groups)
        columns = pl.ds(pl.multiple_of(source * width, width), width)
        out_ref[0, :, columns] = dot(readout_ref[...], part[...]).astype(BF16)


def params(mebibytes):
    return pltpu.CompilerParams(vmem_limit_bytes=mebibytes << 20)


def cost(us):
    return pl.CostEstimate(flops=int(us * 1.1e9), bytes_accessed=int(us * 1e6), transcendentals=0)


def whole(shape):
    return pl.BlockSpec(shape, lambda *a: (0,) * len(shape))


def shards(mesh, queries, keys, values, gates, ridge, out_weight):
    tokens, width = queries.shape
    heads = width // HD
    half = heads // 2
    blocks = tokens // SPAN
    seq, groups = mesh.shape["seq"], mesh.shape["head"]
    columns = out_weight.shape[1]
    side = 4
    place = lax.axis_index("seq")
    core = lax.rem(place, 2)
    x_at = lax.rem(place // 2, side)
    y_at = place // (2 * side)
    group = lax.axis_index("head")
    core_arg = core.reshape(1).astype(jnp.int32)
    group_arg = group.reshape(1).astype(jnp.int32)
    smem = pl.BlockSpec(memory_space=pltpu.SMEM)

    def perm_core():
        return [(p, p ^ 1) for p in range(seq)]

    def perm_x(shift):
        return [(p, (p // 8) * 8 + ((p // 2 + shift) % side) * 2 + p % 2) for p in range(seq)]

    def perm_y(shift):
        return [(p, (p + 8 * shift) % seq) for p in range(seq)]

    def send(array, perm):
        return lax.ppermute(array, "seq", perm)

    def rows_from(shift, weight):
        piece = lax.dynamic_slice_in_dim(weight, lax.rem(group + shift, groups) * width, width, 0)
        return lax.ppermute(piece, "head", [(i, (i + shift) % groups) for i in range(groups)])

    sums = (2 * half, HD, HD)
    by_head = pl.BlockSpec((tokens, HD), lambda h: (0, h))
    head_turned = pl.BlockSpec((1, HD, tokens), lambda h: (h, 0, 0))
    head_blocks = pl.BlockSpec((1, blocks, HD, HD), lambda h: (h, 0, 0, 0))
    row = pl.BlockSpec((1, 1, tokens), lambda h: (h, 0, 0))
    row_shape = jax.ShapeDtypeStruct((heads, 1, tokens), F32)
    turned_shape = jax.ShapeDtypeStruct((heads, HD, tokens), BF16)
    block_shape = jax.ShapeDtypeStruct((heads, blocks, HD, HD), F32)
    by_half = pl.BlockSpec((tokens, half * HD), lambda s: (0, s))
    half_row = pl.BlockSpec((half, 1, tokens), lambda s: (s, 0, 0))
    mine, theirs, keys_turned, scale, gated = pl.pallas_call(
        functools.partial(totals_kernel, half),
        grid=(2,),
        in_specs=[smem, by_half, by_half, whole((heads, tokens))],
        out_specs=[
            whole(sums),
            whole(sums),
            pl.BlockSpec((half, HD, tokens), lambda s: (s, 0, 0)),
            half_row,
            half_row,
        ],
        out_shape=[jax.ShapeDtypeStruct(sums, F32)] * 2 + [turned_shape, row_shape, row_shape],
        compiler_params=params(60),
        cost_estimate=cost(5),
        name="totals",
    )(core_arg, keys, values, gates.T)

    def before_of(parts, at):
        return sum(jnp.where(at >= shift, part.astype(F32), 0.0) for shift, part in enumerate(parts, 1))

    received = send(theirs, perm_core())
    chip = (mine + received).astype(F16)
    chip, keys_turned_later, weight = lax.optimization_barrier((chip, keys_turned, out_weight))
    along = [send(chip, perm_x(shift)) for shift in range(1, side)]
    parts = [rows_from(1, weight)]
    local_gram, local_moment, values_turned = pl.pallas_call(
        functools.partial(local_kernel, blocks),
        grid=(heads,),
        in_specs=[head_turned, row, row, by_head, by_head],
        out_specs=[head_blocks, head_blocks, head_turned],
        out_shape=[block_shape, block_shape, turned_shape],
        compiler_params=params(16),
        cost_estimate=cost(5),
        name="local",
    )(keys_turned_later, scale, gated, keys, values)

    row_total = (chip.astype(F32) + sum(part.astype(F32) for part in along)).astype(F16)
    row_total, queries_later, weight = lax.optimization_barrier((row_total, queries, weight))
    above = [send(row_total, perm_y(shift)) for shift in range(1, side)]
    parts += [rows_from(shift, weight) for shift in range(2, groups - 1)]
    columns_spec = pl.BlockSpec((1, SPAN, SPAN), lambda h: (h, 0, 0))
    columns_shape = jax.ShapeDtypeStruct((heads, SPAN, SPAN), F32)
    queries_turned, scale_columns, gated_columns = pl.pallas_call(
        functools.partial(columns_kernel, blocks),
        grid=(heads,),
        in_specs=[by_head, row, row],
        out_specs=[head_turned, columns_spec, columns_spec],
        out_shape=[turned_shape, columns_shape, columns_shape],
        compiler_params=params(16),
        cost_estimate=cost(3),
        name="columns",
    )(queries_later, scale, gated)

    above, weight = lax.optimization_barrier((above, weight))
    parts.append(rows_from(groups - 1, weight))
    before = before_of(along, x_at) + before_of(above, y_at)
    keep = before + jnp.where(core == 1, received, 0.0)
    give = before + jnp.where(core == 0, mine, 0.0)
    got = send(give, perm_core())

    step_blocks = 4
    step = step_blocks * SPAN
    units = heads * step_blocks
    readout = pl.pallas_call(
        functools.partial(solve_kernel, heads, step_blocks, blocks // step_blocks),
        grid=(blocks // step_blocks,),
        in_specs=[
            smem,
            smem,
        ]
        + [pl.BlockSpec(memory_space=pltpu.VMEM)] * 10,
        out_specs=pl.BlockSpec((step, width), lambda b: (b, 0)),
        out_shape=jax.ShapeDtypeStruct((tokens, width), BF16),
        scratch_shapes=[
            pltpu.VMEM((units, 2 * HD, 2 * HD), BF16),
            pltpu.VMEM((units, HD, 2 * HD), BF16),
            pltpu.VMEM((units, SPAN, SPAN), F32),
            pltpu.VMEM((units, HD, SPAN), F32),
            pltpu.VMEM((units, HD, SPAN), F32),
            pltpu.VMEM((units, HD, SPAN), F32),
            pltpu.VMEM((units, 1, SPAN), F32),
        ],
        compiler_params=params(32),
        cost_estimate=cost(30),
        name="solve",
    )(
        core_arg,
        ridge,
        queries_turned,
        keys,
        keys_turned,
        scale_columns,
        gated_columns,
        local_gram,
        values_turned,
        local_moment,
        keep,
        got,
    )

    step = 2 * SPAN
    out = pl.pallas_call(
        functools.partial(project_kernel, groups),
        grid_spec=pltpu.PrefetchScalarGridSpec(
            num_scalar_prefetch=1,
            grid=(tokens // step,),
            in_specs=[
                pl.BlockSpec((step, width), lambda b, g: (b, 0)),
                pl.BlockSpec((width, columns), lambda b, g: (g[0], 0)),
            ]
            + [pl.BlockSpec(memory_space=pltpu.VMEM)] * (groups - 1),
            out_specs=pl.BlockSpec((1, step, columns * groups), lambda b, g: (0, b, 0)),
        ),
        out_shape=jax.ShapeDtypeStruct((1, tokens, columns * groups), BF16),
        compiler_params=params(12),
        cost_estimate=cost(5),
        name="project",
    )(group_arg, readout, out_weight, *parts)
    return out


def solution(mesh):
    return jax.shard_map(
        functools.partial(shards, mesh),
        mesh=mesh,
        in_specs=(
            P("seq", "head"),
            P("seq", "head"),
            P("seq", "head"),
            P("seq", "head"),
            P("head"),
            P(None, "head"),
        ),
        out_specs=P("head", "seq", None),
        check_vma=False,
    )
```

```python
import functools
import jax
import jax.numpy as jnp
from jax import lax
from jax.experimental import pallas as pl
from jax.experimental.pallas import tpu as pltpu
from jax.sharding import PartitionSpec as P

HD = 128
SPAN = 128
ITERS = 8
EPS = 1e-06
F32 = jnp.float32
BF16 = jnp.bfloat16
F16 = jnp.float16
SHRINK = 16.0
LAG = 4


def two_terms(value):
    high = value.astype(BF16)
    return high, (value - high.astype(F32)).astype(BF16)


def dot(left, right):
    return jnp.dot(left, right, preferred_element_type=F32)


def head_cols(head):
    return slice(head * HD, (head + 1) * HD)


def totals_kernel(
    half, core_ref, keys_ref, values_ref, gates_ref, mine_ref, theirs_ref, turned_ref, factors_ref
):
    step = pl.program_id(0)
    lefts = []
    for head in range(half):
        turned = keys_ref[:, head_cols(head)].T
        turned_ref[head] = turned
        wide = turned.astype(F32)
        norm = jnp.sum(wide * wide, axis=0, keepdims=True) + EPS
        gate = gates_ref[pl.ds(step * half + head, 1), :]
        scale = gate / norm
        gated = gate * lax.rsqrt(norm)
        factors_ref[head] = jnp.concatenate([scale, gated], axis=0)
        for factor in (scale, gated * (1.0 / SHRINK)):
            lefts.append(jnp.concatenate(two_terms(wide * factor), axis=0))
    grams = [dot(lefts[2 * head], keys_ref[:, head_cols(head)]) for head in range(half)]
    moments = [dot(lefts[2 * head + 1], values_ref[:, head_cols(head)]) for head in range(half)]
    sums = [product[:HD] + product[HD:] for product in grams + moments]
    own = core_ref[0] == step

    @pl.when(own)
    def _():
        for at, value in enumerate(sums):
            mine_ref[at] = value

    @pl.when(jnp.logical_not(own))
    def _():
        for at, value in enumerate(sums):
            theirs_ref[at] = value


def local_kernel(blocks, tag_ref, turned_ref, factors_ref, keys_ref, values_ref, gram_ref, moment_ref, values_turned_ref):
    values_turned_ref[0] = values_ref[...].T
    gram_ref[0, 0] = jnp.zeros((HD, HD), F32)
    moment_ref[0, 0] = jnp.zeros((HD, HD), F32)
    grams, moments = [], []
    for block in range(blocks - 1):
        span = slice(block * SPAN, (block + 1) * SPAN)
        keys = turned_ref[0, :, span].astype(F32)
        left = jnp.concatenate(two_terms(keys * factors_ref[0, :1, span]), axis=0)
        grams.append(dot(left, keys_ref[span, :]))
        left = jnp.concatenate(two_terms(keys * factors_ref[0, 1:, span]), axis=0)
        moments.append(dot(left, values_ref[span, :]))
    for block in range(blocks - 1):
        gram, moment = grams[block], moments[block]
        gram_ref[0, block + 1] = gram_ref[0, block] + (gram[:HD] + gram[HD:])
        moment_ref[0, block + 1] = moment_ref[0, block] + (moment[:HD] + moment[HD:]).T


def columns_kernel(blocks, queries_ref, factors_ref, turned_ref, scale_ref, gated_ref):
    turned_ref[0] = queries_ref[...].T
    for at, out_ref in enumerate((scale_ref, gated_ref)):
        spans = [factors_ref[0, at : at + 1, block * SPAN : (block + 1) * SPAN] for block in range(blocks)]
        spans += [jnp.zeros((1, SPAN), F32)] * (SPAN - blocks)
        out_ref[0] = jnp.concatenate(spans, axis=0).T


def solve_kernel(
    heads,
    blocks,
    steps,
    core_ref,
    ridge_ref,
    queries_ref,
    keys_ref,
    turned_ref,
    scale_ref,
    gated_ref,
    local_ref,
    values_ref,
    local_moment_ref,
    keep_ref,
    got_ref,
    readout_ref,
    first,
    second,
    masks,
    xs,
    rs,
    ds,
    norms,
):
    core = core_ref[0]
    row = lax.broadcasted_iota(jnp.int32, (SPAN, SPAN), 0)
    column = lax.broadcasted_iota(jnp.int32, (SPAN, SPAN), 1)
    causal = row <= column
    units = [(head, block) for block in range(blocks) for head in range(heads)]
    count = len(units)
    step = pl.program_id(0)

    def column_of(ref, head, block):
        value = ref[head, :, block : block + 1]
        for at in range(1, steps):
            other = at * blocks + block
            value = jnp.where(step == at, ref[head, :, other : other + 1], value)
        return value

    start = pl.multiple_of(step * blocks * SPAN, blocks * SPAN)
    half = heads // 2
    grams, moments = [], []
    for head in range(heads):
        own, at = core == head // half, head % half
        gram = jnp.where(own, keep_ref[at], got_ref[at])
        grams.append(gram + jnp.where(row == column, ridge_ref[head], 0.0))
        moments.append(jnp.where(own, keep_ref[half + at], got_ref[half + at]).T * SHRINK)

    def prepare(unit):
        head, block = units[unit]
        rows = pl.ds(start + block * SPAN, SPAN)
        own = keys_ref[rows, head_cols(head)]
        masks[unit] = jnp.where(causal, column_of(scale_ref, head, block), 0.0)
        high, low = two_terms(grams[head] + local_ref[head, step * blocks + block])
        first[unit, :HD, :HD] = high
        first[unit, :HD, HD:] = high
        first[unit, HD:, :HD] = own
        first[unit, HD:, HD:] = own
        second[unit, :, :HD] = low
        second[unit, :, HD:] = turned_ref[head, :, rows]
        query = queries_ref[head, :, rows].astype(F32)
        query = query * lax.rsqrt(jnp.sum(query * query, axis=0, keepdims=True) + EPS)
        xs[unit] = jnp.zeros((HD, SPAN), F32)
        rs[unit] = query
        ds[unit] = query
        norms[unit] = jnp.sum(query * query, axis=0, keepdims=True)

    def product_of(unit):
        high, low = two_terms(ds[unit])
        return high, dot(first[unit], jnp.concatenate([high, low], axis=0))

    def image_of(unit, high, product):
        corr = (product[HD:] * masks[unit]).astype(BF16)
        return product[:HD] + dot(second[unit], jnp.concatenate([high, corr], axis=0))

    def update(unit, image):
        direction = ds[unit]
        now = norms[unit]
        size = now / (jnp.sum(direction * image, axis=0, keepdims=True) + EPS)
        xs[unit] += size * direction
        residual = rs[unit] - size * image
        rs[unit] = residual
        after = jnp.sum(residual * residual, axis=0, keepdims=True)
        ds[unit] = residual + (after / (now + EPS)) * direction
        norms[unit] = after

    def correlations_of(unit):
        high, low = two_terms(xs[unit])
        return high, low, dot(first[unit, HD:], jnp.concatenate([high, low], axis=0))

    def readout_of(unit, high, low, product):
        head, block = units[unit]
        corr = jnp.where(causal, product * column_of(gated_ref, head, block), 0.0).astype(BF16)
        moment_high, moment_low = two_terms(moments[head] + local_moment_ref[head, step * blocks + block])
        values = values_ref[head, :, pl.ds(start + block * SPAN, SPAN)]
        left = jnp.concatenate([moment_high, moment_high, moment_low, values], axis=1)
        return dot(left, jnp.concatenate([high, low, high, corr], axis=0))

    def store(unit, readout):
        head, block = units[unit]
        readout_ref[block * SPAN : (block + 1) * SPAN, head_cols(head)] = readout.T.astype(BF16)

    solved = ITERS * count
    products, images = {}, {}
    for at in range(solved + count + 2 * LAG):
        if at < count:
            prepare(at)
        if at < solved + count:
            products[at] = product_of(at % count) if at < solved else correlations_of(at % count)
        then = at - LAG
        if 0 <= then < solved + count:
            stage = image_of if then < solved else readout_of
            images[then] = stage(then % count, *products.pop(then))
        then = at - 2 * LAG
        if 0 <= then < solved + count:
            stage = update if then < solved else store
            stage(then % count, images.pop(then))


def project_kernel(groups, group_ref, readout_ref, own_ref, *rest):
    others, out_ref = rest[: groups - 1], rest[groups - 1]
    group = group_ref[0]
    width = own_ref.shape[1]
    for shift, part in enumerate((own_ref,) + tuple(others)):
        source = lax.rem(group + groups - shift, groups)
        columns = pl.ds(pl.multiple_of(source * width, width), width)
        out_ref[0, :, columns] = dot(readout_ref[...], part[...]).astype(BF16)


def params(mebibytes):
    return pltpu.CompilerParams(vmem_limit_bytes=mebibytes << 20)


def cost(us):
    return pl.CostEstimate(flops=int(us * 1.1e9), bytes_accessed=int(us * 1e6), transcendentals=0)


def whole(shape):
    return pl.BlockSpec(shape, lambda *a: (0,) * len(shape))


def shards(mesh, queries, keys, values, gates, ridge, out_weight):
    tokens, width = queries.shape
    heads = width // HD
    half = heads // 2
    blocks = tokens // SPAN
    seq, groups = mesh.shape["seq"], mesh.shape["head"]
    columns = out_weight.shape[1]
    side = 4
    place = lax.axis_index("seq")
    core = lax.rem(place, 2)
    x_at = lax.rem(place // 2, side)
    y_at = place // (2 * side)
    group = lax.axis_index("head")
    core_arg = core.reshape(1).astype(jnp.int32)
    group_arg = group.reshape(1).astype(jnp.int32)
    smem = pl.BlockSpec(memory_space=pltpu.SMEM)

    def perm_core():
        return [(p, p ^ 1) for p in range(seq)]

    def perm_x(shift):
        return [(p, (p // 8) * 8 + ((p // 2 + shift) % side) * 2 + p % 2) for p in range(seq)]

    def perm_y(shift):
        return [(p, (p + 8 * shift) % seq) for p in range(seq)]

    def send(array, perm):
        return lax.ppermute(array, "seq", perm)

    def rows_from(shift, weight):
        piece = lax.dynamic_slice_in_dim(weight, lax.rem(group + shift, groups) * width, width, 0)
        return lax.ppermute(piece, "head", [(i, (i + shift) % groups) for i in range(groups)])

    sums = (2 * half, HD, HD)
    by_head = pl.BlockSpec((tokens, HD), lambda h: (0, h))
    head_turned = pl.BlockSpec((1, HD, tokens), lambda h: (h, 0, 0))
    head_blocks = pl.BlockSpec((1, blocks, HD, HD), lambda h: (h, 0, 0, 0))
    rows = pl.BlockSpec((1, 2, tokens), lambda h: (h, 0, 0))
    rows_shape = jax.ShapeDtypeStruct((heads, 2, tokens), F32)
    turned_shape = jax.ShapeDtypeStruct((heads, HD, tokens), BF16)
    block_shape = jax.ShapeDtypeStruct((heads, blocks, HD, HD), F32)
    by_half = pl.BlockSpec((tokens, half * HD), lambda s: (0, s))
    mine, theirs, keys_turned, factors = pl.pallas_call(
        functools.partial(totals_kernel, half),
        grid=(2,),
        in_specs=[smem, by_half, by_half, whole((heads, tokens))],
        out_specs=[
            whole(sums),
            whole(sums),
            pl.BlockSpec((half, HD, tokens), lambda s: (s, 0, 0)),
            pl.BlockSpec((half, 2, tokens), lambda s: (s, 0, 0)),
        ],
        out_shape=[jax.ShapeDtypeStruct(sums, F32)] * 2 + [turned_shape, rows_shape],
        compiler_params=params(60),
        cost_estimate=cost(5),
        name="totals",
    )(core_arg, keys, values, gates.T)

    def before_of(parts, at):
        return sum(jnp.where(at >= shift, part.astype(F32), 0.0) for shift, part in enumerate(parts, 1))

    received = send(theirs, perm_core())
    chip = (mine + received).astype(F16)
    chip, tag, weight = lax.optimization_barrier((chip, core_arg, out_weight))
    along = [send(chip, perm_x(shift)) for shift in range(1, side)]
    parts = [rows_from(1, weight)]
    local_gram, local_moment, values_turned = pl.pallas_call(
        functools.partial(local_kernel, blocks),
        grid=(heads,),
        in_specs=[smem, head_turned, rows, by_head, by_head],
        out_specs=[head_blocks, head_blocks, head_turned],
        out_shape=[block_shape, block_shape, turned_shape],
        compiler_params=params(16),
        cost_estimate=cost(5),
        name="local",
    )(tag, keys_turned, factors, keys, values)

    row_total = (chip.astype(F32) + sum(part.astype(F32) for part in along)).astype(F16)
    row_total, queries_later, weight = lax.optimization_barrier((row_total, queries, weight))
    above = [send(row_total, perm_y(shift)) for shift in range(1, side)]
    parts += [rows_from(shift, weight) for shift in range(2, groups - 1)]
    columns_spec = pl.BlockSpec((1, SPAN, SPAN), lambda h: (h, 0, 0))
    columns_shape = jax.ShapeDtypeStruct((heads, SPAN, SPAN), F32)
    queries_turned, scale_columns, gated_columns = pl.pallas_call(
        functools.partial(columns_kernel, blocks),
        grid=(heads,),
        in_specs=[by_head, rows],
        out_specs=[head_turned, columns_spec, columns_spec],
        out_shape=[turned_shape, columns_shape, columns_shape],
        compiler_params=params(16),
        cost_estimate=cost(3),
        name="columns",
    )(queries_later, factors)

    above, weight = lax.optimization_barrier((above, weight))
    parts.append(rows_from(groups - 1, weight))
    before = before_of(along, x_at) + before_of(above, y_at)
    keep = before + jnp.where(core == 1, received, 0.0)
    give = before + jnp.where(core == 0, mine, 0.0)
    got = send(give, perm_core())

    step_blocks = 4
    step = step_blocks * SPAN
    units = heads * step_blocks
    readout = pl.pallas_call(
        functools.partial(solve_kernel, heads, step_blocks, blocks // step_blocks),
        grid=(blocks // step_blocks,),
        in_specs=[
            smem,
            smem,
        ]
        + [pl.BlockSpec(memory_space=pltpu.VMEM)] * 10,
        out_specs=pl.BlockSpec((step, width), lambda b: (b, 0)),
        out_shape=jax.ShapeDtypeStruct((tokens, width), BF16),
        scratch_shapes=[
            pltpu.VMEM((units, 2 * HD, 2 * HD), BF16),
            pltpu.VMEM((units, HD, 2 * HD), BF16),
            pltpu.VMEM((units, SPAN, SPAN), F32),
            pltpu.VMEM((units, HD, SPAN), F32),
            pltpu.VMEM((units, HD, SPAN), F32),
            pltpu.VMEM((units, HD, SPAN), F32),
            pltpu.VMEM((units, 1, SPAN), F32),
        ],
        compiler_params=params(32),
        cost_estimate=cost(30),
        name="solve",
    )(
        core_arg,
        ridge,
        queries_turned,
        keys,
        keys_turned,
        scale_columns,
        gated_columns,
        local_gram,
        values_turned,
        local_moment,
        keep,
        got,
    )

    step = 2 * SPAN
    out = pl.pallas_call(
        functools.partial(project_kernel, groups),
        grid_spec=pltpu.PrefetchScalarGridSpec(
            num_scalar_prefetch=1,
            grid=(tokens // step,),
            in_specs=[
                pl.BlockSpec((step, width), lambda b, g: (b, 0)),
                pl.BlockSpec((width, columns), lambda b, g: (g[0], 0)),
            ]
            + [pl.BlockSpec(memory_space=pltpu.VMEM)] * (groups - 1),
            out_specs=pl.BlockSpec((1, step, columns * groups), lambda b, g: (0, b, 0)),
        ),
        out_shape=jax.ShapeDtypeStruct((1, tokens, columns * groups), BF16),
        compiler_params=params(12),
        cost_estimate=cost(5),
        name="project",
    )(group_arg, readout, out_weight, *parts)
    return out


def solution(mesh):
    return jax.shard_map(
        functools.partial(shards, mesh),
        mesh=mesh,
        in_specs=(
            P("seq", "head"),
            P("seq", "head"),
            P("seq", "head"),
            P("seq", "head"),
            P("head"),
            P(None, "head"),
        ),
        out_specs=P("head", "seq", None),
        check_vma=False,
    )
```

```python
import functools
import jax
import jax.numpy as jnp
from jax import lax
from jax.experimental import pallas as pl
from jax.experimental.pallas import tpu as pltpu
from jax.sharding import PartitionSpec as P

HD = 128
SPAN = 128
ITERS = 8
EPS = 1e-06
F32 = jnp.float32
BF16 = jnp.bfloat16
F16 = jnp.float16
SHRINK = 16.0
LAG = 4


def two_terms(value):
    high = value.astype(BF16)
    return high, (value - high.astype(F32)).astype(BF16)


def dot(left, right):
    return jnp.dot(left, right, preferred_element_type=F32)


def head_cols(head):
    return slice(head * HD, (head + 1) * HD)


def totals_kernel(
    half, core_ref, keys_ref, values_ref, gates_ref, mine_ref, theirs_ref, turned_ref, factors_ref
):
    step = pl.program_id(0)
    lefts = []
    for head in range(half):
        turned = keys_ref[:, head_cols(head)].T
        turned_ref[head] = turned
        wide = turned.astype(F32)
        norm = jnp.sum(wide * wide, axis=0, keepdims=True) + EPS
        gate = gates_ref[pl.ds(step * half + head, 1), :]
        scale = gate / norm
        gated = gate * lax.rsqrt(norm)
        factors_ref[head] = jnp.concatenate([scale, gated], axis=0)
        for factor in (scale, gated * (1.0 / SHRINK)):
            lefts.append(jnp.concatenate(two_terms(wide * factor), axis=0))
    grams = [dot(lefts[2 * head], keys_ref[:, head_cols(head)]) for head in range(half)]
    moments = [dot(lefts[2 * head + 1], values_ref[:, head_cols(head)]) for head in range(half)]
    sums = [product[:HD] + product[HD:] for product in grams + moments]
    own = core_ref[0] == step

    @pl.when(own)
    def _():
        for at, value in enumerate(sums):
            mine_ref[at] = value

    @pl.when(jnp.logical_not(own))
    def _():
        for at, value in enumerate(sums):
            theirs_ref[at] = value


def local_kernel(blocks, tag_ref, factors_ref, keys_ref, values_ref, gram_ref, moment_ref, values_turned_ref):
    values_turned_ref[0] = values_ref[...].T
    gram_ref[0, 0] = jnp.zeros((HD, HD), F32)
    moment_ref[0, 0] = jnp.zeros((HD, HD), F32)
    grams, moments = [], []
    for block in range(blocks - 1):
        span = slice(block * SPAN, (block + 1) * SPAN)
        keys = keys_ref[span, :].T.astype(F32)
        left = jnp.concatenate(two_terms(keys * factors_ref[0, :1, span]), axis=0)
        grams.append(dot(left, keys_ref[span, :]))
        left = jnp.concatenate(two_terms(keys * factors_ref[0, 1:, span]), axis=0)
        moments.append(dot(left, values_ref[span, :]))
    for block in range(blocks - 1):
        gram, moment = grams[block], moments[block]
        gram_ref[0, block + 1] = gram_ref[0, block] + (gram[:HD] + gram[HD:])
        moment_ref[0, block + 1] = moment_ref[0, block] + (moment[:HD] + moment[HD:]).T


def columns_kernel(blocks, queries_ref, factors_ref, turned_ref, scale_ref, gated_ref):
    turned_ref[0] = queries_ref[...].T
    for at, out_ref in enumerate((scale_ref, gated_ref)):
        spans = [factors_ref[0, at : at + 1, block * SPAN : (block + 1) * SPAN] for block in range(blocks)]
        spans += [jnp.zeros((1, SPAN), F32)] * (SPAN - blocks)
        out_ref[0] = jnp.concatenate(spans, axis=0).T


def solve_kernel(
    heads,
    blocks,
    steps,
    core_ref,
    ridge_ref,
    queries_ref,
    keys_ref,
    turned_ref,
    scale_ref,
    gated_ref,
    local_ref,
    values_ref,
    local_moment_ref,
    keep_ref,
    got_ref,
    readout_ref,
    first,
    second,
    masks,
    xs,
    rs,
    ds,
    norms,
):
    core = core_ref[0]
    row = lax.broadcasted_iota(jnp.int32, (SPAN, SPAN), 0)
    column = lax.broadcasted_iota(jnp.int32, (SPAN, SPAN), 1)
    causal = row <= column
    units = [(head, block) for block in range(blocks) for head in range(heads)]
    count = len(units)
    step = pl.program_id(0)

    def column_of(ref, head, block):
        value = ref[head, :, block : block + 1]
        for at in range(1, steps):
            other = at * blocks + block
            value = jnp.where(step == at, ref[head, :, other : other + 1], value)
        return value

    start = pl.multiple_of(step * blocks * SPAN, blocks * SPAN)
    half = heads // 2
    grams, moments = [], []
    for head in range(heads):
        own, at = core == head // half, head % half
        gram = jnp.where(own, keep_ref[at], got_ref[at])
        grams.append(gram + jnp.where(row == column, ridge_ref[head], 0.0))
        moments.append(jnp.where(own, keep_ref[half + at], got_ref[half + at]).T * SHRINK)

    def prepare(unit):
        head, block = units[unit]
        rows = pl.ds(start + block * SPAN, SPAN)
        own = keys_ref[rows, head_cols(head)]
        masks[unit] = jnp.where(causal, column_of(scale_ref, head, block), 0.0)
        high, low = two_terms(grams[head] + local_ref[head, step * blocks + block])
        first[unit, :HD, :HD] = high
        first[unit, :HD, HD:] = high
        first[unit, HD:, :HD] = own
        first[unit, HD:, HD:] = own
        second[unit, :, :HD] = low
        second[unit, :, HD:] = turned_ref[head, :, rows]
        query = queries_ref[head, :, rows].astype(F32)
        query = query * lax.rsqrt(jnp.sum(query * query, axis=0, keepdims=True) + EPS)
        xs[unit] = jnp.zeros((HD, SPAN), F32)
        rs[unit] = query
        ds[unit] = query
        norms[unit] = jnp.sum(query * query, axis=0, keepdims=True)

    def product_of(unit):
        high, low = two_terms(ds[unit])
        return high, dot(first[unit], jnp.concatenate([high, low], axis=0))

    def image_of(unit, high, product):
        corr = (product[HD:] * masks[unit]).astype(BF16)
        return product[:HD] + dot(second[unit], jnp.concatenate([high, corr], axis=0))

    def update(unit, image):
        direction = ds[unit]
        now = norms[unit]
        size = now / (jnp.sum(direction * image, axis=0, keepdims=True) + EPS)
        xs[unit] += size * direction
        residual = rs[unit] - size * image
        rs[unit] = residual
        after = jnp.sum(residual * residual, axis=0, keepdims=True)
        ds[unit] = residual + (after / (now + EPS)) * direction
        norms[unit] = after

    def correlations_of(unit):
        high, low = two_terms(xs[unit])
        return high, low, dot(first[unit, HD:], jnp.concatenate([high, low], axis=0))

    def readout_of(unit, high, low, product):
        head, block = units[unit]
        corr = jnp.where(causal, product * column_of(gated_ref, head, block), 0.0).astype(BF16)
        moment_high, moment_low = two_terms(moments[head] + local_moment_ref[head, step * blocks + block])
        values = values_ref[head, :, pl.ds(start + block * SPAN, SPAN)]
        left = jnp.concatenate([moment_high, moment_high, moment_low, values], axis=1)
        return dot(left, jnp.concatenate([high, low, high, corr], axis=0))

    def store(unit, readout):
        head, block = units[unit]
        readout_ref[block * SPAN : (block + 1) * SPAN, head_cols(head)] = readout.T.astype(BF16)

    solved = ITERS * count
    products, images = {}, {}
    for at in range(solved + count + 2 * LAG):
        if at < count:
            prepare(at)
        if at < solved + count:
            products[at] = product_of(at % count) if at < solved else correlations_of(at % count)
        then = at - LAG
        if 0 <= then < solved + count:
            stage = image_of if then < solved else readout_of
            images[then] = stage(then % count, *products.pop(then))
        then = at - 2 * LAG
        if 0 <= then < solved + count:
            stage = update if then < solved else store
            stage(then % count, images.pop(then))


def project_kernel(groups, group_ref, readout_ref, own_ref, *rest):
    others, out_ref = rest[: groups - 1], rest[groups - 1]
    group = group_ref[0]
    width = own_ref.shape[1]
    for shift, part in enumerate((own_ref,) + tuple(others)):
        source = lax.rem(group + groups - shift, groups)
        columns = pl.ds(pl.multiple_of(source * width, width), width)
        out_ref[0, :, columns] = dot(readout_ref[...], part[...]).astype(BF16)


def params(mebibytes):
    return pltpu.CompilerParams(vmem_limit_bytes=mebibytes << 20)


def cost(us):
    return pl.CostEstimate(flops=int(us * 1.1e9), bytes_accessed=int(us * 1e6), transcendentals=0)


def whole(shape):
    return pl.BlockSpec(shape, lambda *a: (0,) * len(shape))


def shards(mesh, queries, keys, values, gates, ridge, out_weight):
    tokens, width = queries.shape
    heads = width // HD
    half = heads // 2
    blocks = tokens // SPAN
    seq, groups = mesh.shape["seq"], mesh.shape["head"]
    columns = out_weight.shape[1]
    side = 4
    place = lax.axis_index("seq")
    core = lax.rem(place, 2)
    x_at = lax.rem(place // 2, side)
    y_at = place // (2 * side)
    group = lax.axis_index("head")
    core_arg = core.reshape(1).astype(jnp.int32)
    group_arg = group.reshape(1).astype(jnp.int32)
    smem = pl.BlockSpec(memory_space=pltpu.SMEM)

    def perm_core():
        return [(p, p ^ 1) for p in range(seq)]

    def perm_x(shift):
        return [(p, (p // 8) * 8 + ((p // 2 + shift) % side) * 2 + p % 2) for p in range(seq)]

    def perm_y(shift):
        return [(p, (p + 8 * shift) % seq) for p in range(seq)]

    def send(array, perm):
        return lax.ppermute(array, "seq", perm)

    def rows_from(shift, weight):
        piece = lax.dynamic_slice_in_dim(weight, lax.rem(group + shift, groups) * width, width, 0)
        return lax.ppermute(piece, "head", [(i, (i + shift) % groups) for i in range(groups)])

    sums = (2 * half, HD, HD)
    by_head = pl.BlockSpec((tokens, HD), lambda h: (0, h))
    head_turned = pl.BlockSpec((1, HD, tokens), lambda h: (h, 0, 0))
    head_blocks = pl.BlockSpec((1, blocks, HD, HD), lambda h: (h, 0, 0, 0))
    rows = pl.BlockSpec((1, 2, tokens), lambda h: (h, 0, 0))
    rows_shape = jax.ShapeDtypeStruct((heads, 2, tokens), F32)
    turned_shape = jax.ShapeDtypeStruct((heads, HD, tokens), BF16)
    block_shape = jax.ShapeDtypeStruct((heads, blocks, HD, HD), F32)
    by_half = pl.BlockSpec((tokens, half * HD), lambda s: (0, s))
    mine, theirs, keys_turned, factors = pl.pallas_call(
        functools.partial(totals_kernel, half),
        grid=(2,),
        in_specs=[smem, by_half, by_half, whole((heads, tokens))],
        out_specs=[
            whole(sums),
            whole(sums),
            pl.BlockSpec((half, HD, tokens), lambda s: (s, 0, 0)),
            pl.BlockSpec((half, 2, tokens), lambda s: (s, 0, 0)),
        ],
        out_shape=[jax.ShapeDtypeStruct(sums, F32)] * 2 + [turned_shape, rows_shape],
        compiler_params=params(60),
        cost_estimate=cost(5),
        name="totals",
    )(core_arg, keys, values, gates.T)

    def before_of(parts, at):
        return sum(jnp.where(at >= shift, part.astype(F32), 0.0) for shift, part in enumerate(parts, 1))

    received = send(theirs, perm_core())
    chip = (mine + received).astype(F16)
    chip, tag, weight = lax.optimization_barrier((chip, core_arg, out_weight))
    along = [send(chip, perm_x(shift)) for shift in range(1, side)]
    parts = [rows_from(1, weight)]
    local_gram, local_moment, values_turned = pl.pallas_call(
        functools.partial(local_kernel, blocks),
        grid=(heads,),
        in_specs=[smem, rows, by_head, by_head],
        out_specs=[head_blocks, head_blocks, head_turned],
        out_shape=[block_shape, block_shape, turned_shape],
        compiler_params=params(16),
        cost_estimate=cost(5),
        name="local",
    )(tag, factors, keys, values)

    row_total = (chip.astype(F32) + sum(part.astype(F32) for part in along)).astype(F16)
    row_total, queries_later, weight = lax.optimization_barrier((row_total, queries, weight))
    above = [send(row_total, perm_y(shift)) for shift in range(1, side)]
    parts += [rows_from(shift, weight) for shift in range(2, groups - 1)]
    columns_spec = pl.BlockSpec((1, SPAN, SPAN), lambda h: (h, 0, 0))
    columns_shape = jax.ShapeDtypeStruct((heads, SPAN, SPAN), F32)
    queries_turned, scale_columns, gated_columns = pl.pallas_call(
        functools.partial(columns_kernel, blocks),
        grid=(heads,),
        in_specs=[by_head, rows],
        out_specs=[head_turned, columns_spec, columns_spec],
        out_shape=[turned_shape, columns_shape, columns_shape],
        compiler_params=params(16),
        cost_estimate=cost(3),
        name="columns",
    )(queries_later, factors)

    above, weight = lax.optimization_barrier((above, weight))
    parts.append(rows_from(groups - 1, weight))
    before = before_of(along, x_at) + before_of(above, y_at)
    keep = before + jnp.where(core == 1, received, 0.0)
    give = before + jnp.where(core == 0, mine, 0.0)
    got = send(give, perm_core())

    step_blocks = 4
    step = step_blocks * SPAN
    units = heads * step_blocks
    readout = pl.pallas_call(
        functools.partial(solve_kernel, heads, step_blocks, blocks // step_blocks),
        grid=(blocks // step_blocks,),
        in_specs=[
            smem,
            smem,
        ]
        + [pl.BlockSpec(memory_space=pltpu.VMEM)] * 10,
        out_specs=pl.BlockSpec((step, width), lambda b: (b, 0)),
        out_shape=jax.ShapeDtypeStruct((tokens, width), BF16),
        scratch_shapes=[
            pltpu.VMEM((units, 2 * HD, 2 * HD), BF16),
            pltpu.VMEM((units, HD, 2 * HD), BF16),
            pltpu.VMEM((units, SPAN, SPAN), F32),
            pltpu.VMEM((units, HD, SPAN), F32),
            pltpu.VMEM((units, HD, SPAN), F32),
            pltpu.VMEM((units, HD, SPAN), F32),
            pltpu.VMEM((units, 1, SPAN), F32),
        ],
        compiler_params=params(32),
        cost_estimate=cost(30),
        name="solve",
    )(
        core_arg,
        ridge,
        queries_turned,
        keys,
        keys_turned,
        scale_columns,
        gated_columns,
        local_gram,
        values_turned,
        local_moment,
        keep,
        got,
    )

    step = 2 * SPAN
    out = pl.pallas_call(
        functools.partial(project_kernel, groups),
        grid_spec=pltpu.PrefetchScalarGridSpec(
            num_scalar_prefetch=1,
            grid=(tokens // step,),
            in_specs=[
                pl.BlockSpec((step, width), lambda b, g: (b, 0)),
                pl.BlockSpec((width, columns), lambda b, g: (g[0], 0)),
            ]
            + [pl.BlockSpec(memory_space=pltpu.VMEM)] * (groups - 1),
            out_specs=pl.BlockSpec((1, step, columns * groups), lambda b, g: (0, b, 0)),
        ),
        out_shape=jax.ShapeDtypeStruct((1, tokens, columns * groups), BF16),
        compiler_params=params(12),
        cost_estimate=cost(5),
        name="project",
    )(group_arg, readout, out_weight, *parts)
    return out


def solution(mesh):
    return jax.shard_map(
        functools.partial(shards, mesh),
        mesh=mesh,
        in_specs=(
            P("seq", "head"),
            P("seq", "head"),
            P("seq", "head"),
            P("seq", "head"),
            P("head"),
            P(None, "head"),
        ),
        out_specs=P("head", "seq", None),
        check_vma=False,
    )
```
